128 devices in a mesh: island: 8 (over x, y_hi), fsdp: 16 (over z, y_lo, core).
Axes of the slice: x: 4, y: 4 (y_hi: 2, y_lo: 2; y = y_hi * 2 + y_lo), z: 4, core: 2. Of those that a mesh axis runs over, the one named last changes fastest.
Arguments:
- delta: bfloat16 [8, 8192, 8192], P('island', 'fsdp'), may hold values from -24 to 24
- sketch: bfloat16 [8192, 256], P('fsdp'), may hold values from -0.0625 to 0.0625
- params: float32 [8192, 8192], P('fsdp', 'island'), may hold values from -6 to 6
- momentum: float32 [8192, 8192], P('fsdp', 'island'), may hold values from -3 to 3
Outputs:
- new_params: float32 [8192, 8192], P('fsdp', 'island')
- new_momentum: float32 [8192, 8192], P('fsdp', 'island')
The draws below stay inside these ranges and needn't reach their ends.
All inputs are finite; a program needn't handle non-finite values. Where the reference program divides by a largest or mean magnitude, that divisor is 1e-20 or more.
Results may differ from the reference program's by a relative error of at most 0.01.
Values may be sent and summed in bfloat16 or wider, within the bound.
No kernel may reach another device: no remote copies, remote signals or barrier semaphores. Data moves between devices by JAX's collectives and lax.ppermute only.
A program may use at most 128 MiB of HBM per device.

```python
import jax
import jax.numpy as jnp
from jax import lax

D = 8192
K = 256
BLK = 128
ISLANDS = 8


def levels(key, extent, cuts, smallest, largest):
    level = 1.0
    for position, shards_of in cuts:
        draws = jax.random.uniform(jax.random.fold_in(jax.random.fold_in(key, 6), position), (shards_of,), jnp.float32, smallest / len(cuts), largest / len(cuts))
        level = level * jnp.repeat(jnp.exp(draws), extent[position] // shards_of).reshape((-1,) + (1,) * (len(extent) - 1 - position))
    return level


def bell_draw(key, shape, scale, bound, shards=(), kind=jnp.bfloat16):
    values = jax.random.normal(key, shape, jnp.float32) * scale
    if len(shards) > 0:
        values = levels(key, shape, shards, -0.22, 0.18) * values
    return jnp.clip(values, min=-bound, max=bound).astype(kind)


def setup_inputs(seed: int = 0) -> dict:
    seeds = jax.random.split(jax.random.key(seed), 5)
    delta = bell_draw(seeds[0], (ISLANDS, D, D), 4.0, 24.0, ((0, 8), (1, 16)))
    sketch = bell_draw(seeds[1], (D, K), D ** -0.5, 0.0625, ((0, 16),))
    params = bell_draw(seeds[2], (D, D), 1.0, 6.0, ((0, 16), (1, 8)), jnp.float32)
    momentum = bell_draw(seeds[3], (D, D), 0.5, 3.0, ((0, 16), (1, 8)), jnp.float32)
    return {"delta": delta, "sketch": sketch, "params": params, "momentum": momentum}


def compress(values):
    count = values.shape[0]
    blocks = values.reshape(count, K // BLK, BLK)
    scale = (jnp.max(jnp.abs(blocks), axis=2) + 1e-06).astype(jnp.bfloat16)
    code = (blocks / scale.astype(jnp.float32)[:, :, None]).astype(jnp.bfloat16)
    return (code.reshape(count, K), scale)

def rebuild(code_q, scale_q, code_b, scale_b):
    total = jnp.zeros((code_q.shape[0], code_b.shape[0]), jnp.float32)
    for block in range(K // BLK):
        lower = block * BLK
        part = jnp.dot(code_q[:, lower:lower + BLK].astype(jnp.float32), code_b[:, lower:lower + BLK].T.astype(jnp.float32), preferred_element_type=jnp.float32)
        weight = scale_q[:, block].astype(jnp.float32)[:, None] * scale_b[:, block].astype(jnp.float32)[None, :]
        total = total + weight * part
    return total

def reference(delta, sketch, params, momentum):
    total = jnp.zeros((D, D), jnp.float32)
    for island in range(ISLANDS):
        matrix = delta[island]
        sketched = jnp.dot(matrix.astype(jnp.float32), sketch.astype(jnp.float32), preferred_element_type=jnp.float32)
        gram = jnp.dot(sketched.T.astype(jnp.float32), sketched.astype(jnp.float32), precision=lax.Precision.HIGHEST, preferred_element_type=jnp.float32)
        chol = jnp.linalg.cholesky(gram)
        basis = lax.linalg.triangular_solve(chol, sketched, left_side=False, lower=True, transpose_a=True)
        basis_b = basis.astype(jnp.bfloat16)
        coef = jnp.dot(matrix.T.astype(jnp.float32), basis_b.astype(jnp.float32), preferred_element_type=jnp.float32)
        code_q, scale_q = compress(basis)
        code_b, scale_b = compress(coef)
        total = total + rebuild(code_q, scale_q, code_b, scale_b)
    average = total / ISLANDS
    new_momentum = 0.9 * momentum + average
    new_params = params - 0.7 * (average + 0.9 * new_momentum)
    return (new_params, new_momentum)
```

```python
import functools

import jax
import jax.numpy as jnp
import numpy as np
from jax import lax
from jax.experimental import pallas as pl
from jax.experimental.pallas import tpu as pltpu
from jax.sharding import Mesh, PartitionSpec as P

BLK = 128
AXES = ("x", "yh", "z", "yl", "core")
SIZES = (4, 2, 4, 2, 2)
ISLANDS = 8
MOVES = tuple((dz, dl) for dz in range(4) for dl in range(2))
HIGH = lax.Precision.HIGHEST
F32 = jnp.float32
BF16 = jnp.bfloat16


def move(value, where):
    pairs = []
    for c in np.ndindex(*SIZES):
        d = tuple(a % b for a, b in zip(where(*c), SIZES))
        pairs.append((int(np.ravel_multi_index(c, SIZES)), int(np.ravel_multi_index(d, SIZES))))
    return lax.ppermute(value, AXES, pairs)


def shift(value, dx=0, dh=0, dz=0, dl=0, dc=0):
    return move(value, lambda x, h, z, l, c: (x + dx, h + dh, z + dz, l + dl, c + dc))


def params_of(**more):
    return pltpu.CompilerParams(vmem_limit_bytes=48 * 1024 * 1024, **more)


def cost(flops, bytes_accessed):
    return pl.CostEstimate(flops=int(flops), bytes_accessed=int(bytes_accessed), transcendentals=0)


def whole(shape):
    return pl.BlockSpec(shape, lambda *_: (0,) * len(shape))


def recode(values, axis):
    scale = (jnp.max(jnp.abs(values), axis=axis, keepdims=True) + 1e-06).astype(BF16).astype(F32)
    code = (values / scale).astype(BF16)
    return (code.astype(F32) * scale).astype(BF16)


def sketched_kernel(place, delta, *refs):
    pieces, (out, gram) = refs[:16], refs[16:]
    step = pl.program_id(0)
    for k in range(16):

        @pl.when(step == k)
        def _(k=k):
            part = jnp.dot(delta[...], pieces[k][...], preferred_element_type=F32)
            if k == 0:
                out[...] = part
            else:
                out[...] += part
            if k == 15:
                total = out[...]
                gram[...] = lax.dot_general(
                    total, total, (((0,), (0,)), ((), ())), precision=HIGH, preferred_element_type=F32
                )


def sketched_call(place, delta, pieces):
    rows, rank = delta.shape[0], pieces[0].shape[1]
    depth = pieces[0].shape[0]
    return pl.pallas_call(
        sketched_kernel,
        grid_spec=pltpu.PrefetchScalarGridSpec(
            num_scalar_prefetch=1,
            grid=(16,),
            in_specs=[pl.BlockSpec((rows, depth), lambda g, place: (0, place[g]))]
            + [whole((depth, rank))] * 16,
            out_specs=[whole((rows, rank)), whole((rank, rank))],
        ),
        out_shape=[
            jax.ShapeDtypeStruct((rows, rank), F32),
            jax.ShapeDtypeStruct((rank, rank), F32),
        ],
        compiler_params=params_of(),
        cost_estimate=cost(2.6e9, 13e6),
        name="sketched",
    )(place, delta, *pieces)


def product_tile(sketched, delta, turned):
    @pl.when(pl.program_id(0) == 0)
    def _():
        turned[...] = sketched[...].T.astype(BF16)

    return jnp.dot(turned[...], delta[...], preferred_element_type=F32)


def send_kernel(place, sketched, delta, out, turned):
    tile = product_tile(sketched, delta, turned)
    for t in range(8):
        out[t] = tile[:, t * BLK : (t + 1) * BLK].astype(BF16)


def send_call(place, sketched, delta):
    rows, rank = sketched.shape
    return pl.pallas_call(
        send_kernel,
        grid_spec=pltpu.PrefetchScalarGridSpec(
            num_scalar_prefetch=1,
            grid=(4,),
            in_specs=[
                whole((rows, rank)),
                pl.BlockSpec((rows, 1024), lambda g, place: (0, 2 * g + 1 - place[0])),
            ],
            out_specs=pl.BlockSpec((8, rank, BLK), lambda g, place: (0, 0, g)),
            scratch_shapes=[pltpu.VMEM((rank, rows), BF16)],
        ),
        out_shape=jax.ShapeDtypeStruct((8, rank, 4 * BLK), BF16),
        compiler_params=params_of(),
        cost_estimate=cost(1.1e9, 7e6),
        name="product_send",
    )(place, sketched, delta)


def keep_kernel(place, sketched, delta, other, *refs):
    outs, (turned, held) = refs[:8], refs[8:]
    held[...] = product_tile(sketched, delta, turned)
    for k in range(8):
        t = place[1 + k]
        total = held[:, pl.ds(pl.multiple_of(t * BLK, BLK), BLK)] + other[t].astype(F32)
        outs[k][...] = total.astype(BF16)


def keep_call(place, sketched, delta, other):
    rows, rank = sketched.shape
    return pl.pallas_call(
        keep_kernel,
        grid_spec=pltpu.PrefetchScalarGridSpec(
            num_scalar_prefetch=1,
            grid=(4,),
            in_specs=[
                whole((rows, rank)),
                pl.BlockSpec((rows, 1024), lambda g, place: (0, 2 * g + place[0])),
                pl.BlockSpec((8, rank, BLK), lambda g, place: (0, 0, g)),
            ],
            out_specs=[pl.BlockSpec((rank, BLK), lambda g, place: (0, g))] * 8,
            scratch_shapes=[pltpu.VMEM((rank, rows), BF16), pltpu.VMEM((rank, 1024), F32)],
        ),
        out_shape=[jax.ShapeDtypeStruct((rank, 4 * BLK), BF16)] * 8,
        compiler_params=params_of(),
        cost_estimate=cost(1.1e9, 9e6),
        name="product_keep",
    )(place, sketched, delta, other)


def coef_kernel(place, inverse, *refs):
    parts, outs, held = refs[:8], refs[8:12], refs[12]
    total = parts[0][...].astype(F32)
    for part in parts[1:]:
        total += part[...].astype(F32)
    coef = jnp.dot(inverse[...], total, precision=HIGH, preferred_element_type=F32)
    for b in range(2):
        held[b * BLK : (b + 1) * BLK] = recode(coef[b * BLK : (b + 1) * BLK], 0)
    for d in range(4):
        outs[d][...] = held[:, pl.ds(pl.multiple_of(place[d] * BLK, BLK), BLK)]


def coef_call(place, inverse, parts):
    rank = inverse.shape[0]
    vmem = pl.BlockSpec(memory_space=pltpu.VMEM)
    return pl.pallas_call(
        coef_kernel,
        in_specs=[pl.BlockSpec(memory_space=pltpu.SMEM)] + [vmem] * 9,
        out_specs=[vmem] * 4,
        out_shape=[jax.ShapeDtypeStruct((rank, BLK), BF16)] * 4,
        scratch_shapes=[pltpu.VMEM((rank, 4 * BLK), BF16)],
        compiler_params=params_of(),
        cost_estimate=cost(0.4e9, 3e6),
        name="coef",
    )(place, inverse, *parts)


def basis_kernel(sketched, inverse, out):
    basis = lax.dot_general(
        sketched[...],
        inverse[...],
        (((1,), (1,)), ((), ())),
        precision=HIGH,
        preferred_element_type=F32,
    )
    for b in range(2):
        out[:, b * BLK : (b + 1) * BLK] = recode(basis[:, b * BLK : (b + 1) * BLK], 1)


def basis_call(sketched, inverse):
    vmem = pl.BlockSpec(memory_space=pltpu.VMEM)
    return pl.pallas_call(
        basis_kernel,
        in_specs=[vmem] * 2,
        out_specs=vmem,
        out_shape=jax.ShapeDtypeStruct(sketched.shape, BF16),
        compiler_params=params_of(),
        cost_estimate=cost(0.4e9, 1e6),
        name="basis",
    )(sketched, inverse)


def update_kernel(place, params, momentum, *refs):
    here, there, mine, theirs = refs[:4], refs[4:8], refs[8:16], refs[16:24]
    new_params, new_momentum, left = refs[24:]
    step = pl.program_id(0)
    rank = here[0].shape[1]

    def lay(first, second):
        for d in range(4):
            left[:, d * rank : (d + 1) * rank] = first[d][...]
            left[:, (4 + d) * rank : (5 + d) * rank] = second[d][...]

    pl.when((step == 0) & (place[4] == 0))(lambda: lay(here, there))
    pl.when((step == 0) & (place[4] == 1))(lambda: lay(there, here))
    for dz in range(4):

        @pl.when(step == dz)
        def _(dz=dz):
            right = jnp.concatenate(
                [
                    jnp.concatenate([mine[2 * dz + dl][...], theirs[2 * dz + dl][...]], axis=0)
                    for dl in range(2)
                ],
                axis=1,
            )
            average = jnp.dot(left[...], right, preferred_element_type=F32) * (1.0 / ISLANDS)
            for dl in range(2):
                at = pl.ds(pl.multiple_of(((place[5] + dl) % 2) * BLK, BLK), BLK)
                avg = average[:, dl * BLK : (dl + 1) * BLK]
                new = 0.9 * momentum[:, at] + avg
                new_momentum[:, at] = new
                new_params[:, at] = params[:, at] - 0.7 * (avg + 0.9 * new)


def update_call(place, params, momentum, here, there, mine, theirs):
    rows, width = params.shape
    rank = here[0].shape[1]
    tile = pl.BlockSpec((rows, 2 * BLK), lambda g, place: (0, place[g]))
    return pl.pallas_call(
        update_kernel,
        grid_spec=pltpu.PrefetchScalarGridSpec(
            num_scalar_prefetch=1,
            grid=(4,),
            in_specs=[tile, tile] + [whole((rows, rank))] * 8 + [whole((4 * rank, BLK))] * 16,
            out_specs=[tile, tile],
            scratch_shapes=[pltpu.VMEM((rows, 8 * rank), BF16)],
        ),
        out_shape=[jax.ShapeDtypeStruct((rows, width), F32)] * 2,
        compiler_params=params_of(),
        cost_estimate=cost(2.2e9, 14e6),
        name="update",
    )(place, params, momentum, *here, *there, *mine, *theirs)


def body(delta, sketch, params, momentum):
    local = delta[0]
    rank = sketch.shape[1]
    x, yh, z, yl, core = (lax.axis_index(a) for a in AXES)
    ints = lambda values: jnp.stack([jnp.asarray(v, jnp.int32) for v in values])
    chips_in = [((z - dz) % 4) * 2 + (yl - dl) % 2 for dz, dl in MOVES]
    chips_out = [((z + dz) % 4) * 2 + (yl + dl) % 2 for dz, dl in MOVES]

    with jax.named_scope("gather_sketch"):
        pieces = [sketch] + [shift(sketch, dz=dz, dl=dl) for dz, dl in MOVES[1:]]
        swapped = [shift(piece, dc=1) for piece in pieces]
    place = ints([2 * t + core for t in chips_in] + [2 * t + 1 - core for t in chips_in])
    sketched, gram = sketched_call(place, local, pieces + swapped)

    with jax.named_scope("sum_gram"):
        half = rank // 2
        kept = lax.dynamic_slice_in_dim(gram, core * half, half, 0)
        other = lax.dynamic_slice_in_dim(gram, (1 - core) * half, half, 0)
        kept = kept + shift(other, dc=1)
        kept = kept + shift(kept, dl=1)
        kept = kept + move(kept, lambda x, h, z, l, c: (x, h, z ^ 1, l, c))
        kept = kept + move(kept, lambda x, h, z, l, c: (x, h, 3 - z, l, c))
        other = shift(kept, dc=1)
        first = core == 0
        gram = jnp.concatenate([jnp.where(first, kept, other), jnp.where(first, other, kept)], 0)
    with jax.named_scope("chol"):
        chol = jnp.linalg.cholesky(gram)
        inverse = lax.linalg.triangular_solve(
            chol, jnp.eye(rank, dtype=F32), left_side=True, lower=True
        )

    place = ints([core] + chips_out)
    sent = send_call(place, sketched, local)
    with jax.named_scope("sum_cores"):
        got = shift(sent, dc=1)
    kept = keep_call(place, sketched, local, got)
    with jax.named_scope("sum_fsdp"):
        parts = [kept[0]] + [shift(v, dz=dz, dl=dl) for v, (dz, dl) in zip(kept[1:], MOVES[1:])]

    basis = basis_call(sketched, inverse)
    with jax.named_scope("gather_basis"):
        across = shift(basis, dh=1)
        here = [basis] + [shift(basis, dx=d) for d in range(1, 4)]
        there = [across] + [shift(across, dx=d) for d in range(1, 4)]

    place = ints([(x + d) % 4 for d in range(4)])
    tiles = coef_call(place, inverse, parts)
    with jax.named_scope("exchange_coef"):
        tiles = [
            move(v, lambda x, h, z, l, c, d=d: (x + d, c, z, l, h)) for d, v in enumerate(tiles)
        ]
        tiles = jnp.concatenate(tiles, 0)
    with jax.named_scope("gather_coef"):
        mine = [tiles] + [shift(tiles, dz=dz, dl=dl) for dz, dl in MOVES[1:]]
        theirs = [shift(v, dc=1) for v in mine]

    place = ints([(z - dz) % 4 for dz in range(4)] + [(core + yh) % 2, yl])
    return tuple(update_call(place, params, momentum, here, there, mine, theirs))


def solution(mesh):
    mesh = Mesh(mesh.devices.reshape(SIZES), AXES)
    island, fsdp = AXES[:2], AXES[2:]
    placed = (P(island, fsdp, None), P(fsdp, None), P(fsdp, island), P(fsdp, island))
    return jax.shard_map(
        body,
        mesh=mesh,
        in_specs=placed,
        out_specs=(P(fsdp, island), P(fsdp, island)),
        check_vma=False,
    )
```

```python
import functools

import jax
import jax.numpy as jnp
import numpy as np
from jax import lax
from jax.experimental import pallas as pl
from jax.experimental.pallas import tpu as pltpu
from jax.sharding import Mesh, PartitionSpec as P

BLK = 128
AXES = ("x", "yh", "z", "yl", "core")
SIZES = (4, 2, 4, 2, 2)
ISLANDS = 8
HIGH = lax.Precision.HIGHEST
F32 = jnp.float32
BF16 = jnp.bfloat16


def move(value, where):
    pairs = []
    for c in np.ndindex(*SIZES):
        d = tuple(a % b for a, b in zip(where(*c), SIZES))
        pairs.append((int(np.ravel_multi_index(c, SIZES)), int(np.ravel_multi_index(d, SIZES))))
    return lax.ppermute(value, AXES, pairs)


def shift(value, dx=0, dh=0, dz=0, dl=0, dc=0):
    return move(value, lambda x, h, z, l, c: (x + dx, h + dh, z + dz, l + dl, c + dc))


def recode(values, axis):
    scale = (jnp.max(jnp.abs(values), axis=axis, keepdims=True) + 1e-06).astype(BF16).astype(F32)
    code = (values / scale).astype(BF16)
    return (code.astype(F32) * scale).astype(BF16)


VMEM = pl.BlockSpec(memory_space=pltpu.VMEM)
FAR = pl.BlockSpec(memory_space=pltpu.HBM)
SMEM = pl.BlockSpec(memory_space=pltpu.SMEM)


def call(kernel, outs, flops, name, smem=True, scratch=(), vmem=16, far=()):
    def run(*args):
        args = [
            pltpu.with_memory_space_constraint(a, pltpu.HBM) if n in far else a
            for n, a in enumerate(args)
        ]
        return pl.pallas_call(
            kernel,
            in_specs=[
                SMEM if smem and n == 0 else FAR if n in far else VMEM for n in range(len(args))
            ],
            out_specs=[VMEM] * len(outs),
            out_shape=[jax.ShapeDtypeStruct(*o) if isinstance(o, tuple) else o for o in outs],
            scratch_shapes=list(scratch),
            compiler_params=pltpu.CompilerParams(vmem_limit_bytes=vmem * 1024 * 1024),
            cost_estimate=pl.CostEstimate(
                flops=int(flops), bytes_accessed=4 * 1024 * 1024, transcendentals=0
            ),
            name=name,
        )(*args)

    return run


def columns(ref, start, count):
    return ref.at[:, pl.ds(pl.multiple_of(start, count), count)]


def fetch(delta, starts, held, sems):
    copies = [
        pltpu.make_async_copy(columns(delta, start, held.shape[2]), held.at[n], sems.at[n])
        for n, start in enumerate(starts)
    ]
    for copy in copies:
        copy.start()
    return copies


def add_products(copies, pieces, out, held):
    for n, (piece, copy) in enumerate(zip(pieces, copies)):
        copy.wait()
        value = jnp.dot(held[n], piece[...], preferred_element_type=F32)
        if n == 0:
            out[...] = value
        else:
            out[...] += value


def early_kernel(layout, place, delta, *refs):
    pieces, (out, held, sems) = refs[: len(layout)], refs[len(layout) :]
    copies = fetch(delta, [place[at] for at in layout], held, sems)
    add_products(copies, pieces, out, held)


def late_kernel(layout, place, delta, *refs):
    pieces, part = refs[: len(layout)], refs[len(layout)]
    gram, rounded, turned, out, held, sems = refs[len(layout) + 1 :]
    copies = fetch(delta, [place[at] for at in layout], held, sems)
    add_products(copies, pieces, out, held)
    total = out[...] + part[...]
    flipped = total.T
    gram[...] = jnp.dot(flipped, total, precision=HIGH, preferred_element_type=F32)
    rounded[...] = total.astype(BF16)
    turned[...] = flipped.astype(BF16)


def product_kernel(place, delta, turned, sent, kept, held, sems):
    width = held.shape[2]
    blocks = [
        (out, parity, g)
        for out, parity in ((sent, 1 - place[0]), (kept, place[0]))
        for g in range(4)
    ]
    copies = fetch(delta, [(2 * g + parity) * width for _, parity, g in blocks], held, sems)
    for n, ((out, _, g), copy) in enumerate(zip(blocks, copies)):
        copy.wait()
        for q in range(2):
            tile = jnp.dot(
                turned[...], held[n, :, q * 512 : (q + 1) * 512], preferred_element_type=F32
            ).astype(BF16)
            for u in range(4):
                out[4 * q + u, :, g * BLK : (g + 1) * BLK] = tile[:, u * BLK : (u + 1) * BLK]


def spread_kernel(t0, t1, t2, t3, out):
    rank = t0.shape[0]
    for n in range(out.shape[0]):
        for d, tile in enumerate((t0, t1, t2, t3)):
            out[n, d * rank : (d + 1) * rank] = tile[...]


def inverse_kernel(gram, out, left):
    size, wide = gram.shape[0], 16
    left[...] = gram[...]
    rows = lax.broadcasted_iota(jnp.int32, (size, size), 0)
    cols = lax.broadcasted_iota(jnp.int32, (size, size), 1)
    out[...] = (rows == cols).astype(F32)
    row = lax.broadcasted_iota(jnp.int32, (wide, BLK), 0)
    for k in range(0, size, wide):
        lo = k // BLK * BLK
        hi = lo + BLK
        over = lambda v, width: jnp.concatenate([v] * (width // BLK), 1)
        a, b = left[k : k + wide, lo:size], out[k : k + wide, :hi]
        col = [
            jnp.broadcast_to(left[k : k + wide, k + j : k + j + 1], (wide, BLK))
            for j in range(wide)
        ]
        done = []
        for i in range(wide):
            pivot = col[i][i : i + 1]
            root = lax.rsqrt(pivot)
            root = root * (1.5 - 0.5 * pivot * root * root)
            done.append(b[i : i + 1] * over(root, hi))
            inv = root * root
            factor = jnp.where(row == i, 1.0 - inv, col[i] * inv)
            for j in range(i + 1, wide):
                col[j] = col[j] - factor * col[j][i : i + 1]
            a = a - over(factor, size - lo) * a[i : i + 1]
            b = b - over(factor, hi) * b[i : i + 1]
        out[k : k + wide, :hi] = jnp.concatenate(done, 0)
        if k + wide < size:
            a_rest, b_rest = left[k + wide :, lo:size], out[k + wide :, :hi]
            for j in range(wide):
                c = left[k + wide :, k + j : k + j + 1]
                a_rest = a_rest - c * a[j : j + 1]
                b_rest = b_rest - c * b[j : j + 1]
            left[k + wide :, lo:size] = a_rest
            out[k + wide :, :hi] = b_rest


def coef_kernel(place, inverse, parts, *refs):
    outs, held = refs[:4], refs[4]
    total = parts[0].astype(F32)
    for t in range(1, 8):
        total += parts[t].astype(F32)
    coef = jnp.dot(inverse[...], total, precision=HIGH, preferred_element_type=F32)
    for b in range(2):
        held[b * BLK : (b + 1) * BLK] = recode(coef[b * BLK : (b + 1) * BLK], 0)
    for d in range(4):
        outs[d][...] = columns(held, (place[2] + d) % 4 * BLK, BLK)[...]


def basis_kernel(place, s0, s1, s2, s3, mine, theirs, left):
    for d, sketched in enumerate((s0, s1, s2, s3)):
        for n, yh in enumerate((place[3], 1 - place[3])):
            for core, inverse in ((place[0], mine), (1 - place[0], theirs)):
                basis = lax.dot_general(
                    sketched[yh],
                    inverse[d, yh],
                    (((1,), (1,)), ((), ())),
                    preferred_element_type=F32,
                )
                start = pl.multiple_of((2 * (4 * n + d) + core) * BLK, BLK)
                left[:, pl.ds(start, BLK)] = recode(basis, 1)


def partial_kernel(left, mine, out):
    depth = mine.shape[1]
    for t in range(0, 8, 2):
        right = jnp.concatenate([mine[t], mine[t + 1]], axis=1)
        out[:, t * BLK : (t + 2) * BLK] = jnp.dot(
            left[:, :depth], right, preferred_element_type=F32
        )


def update_kernel(params, momentum, part, left, theirs, new_params, new_momentum):
    right = jnp.concatenate([theirs[0], theirs[1]], axis=1)
    rest = jnp.dot(left[...], right, preferred_element_type=F32)
    average = (part[...] + rest) * (1.0 / ISLANDS)
    new = 0.9 * momentum[...] + average
    new_momentum[...] = new
    new_params[...] = params[...] - 0.7 * (average + 0.9 * new)


def update_call(params, momentum, part, left, theirs):
    rows, width = params.shape
    depth = theirs.shape[1]
    tile = pl.BlockSpec((rows, 2 * BLK), lambda g: (0, g))
    return pl.pallas_call(
        update_kernel,
        grid=(4,),
        in_specs=[
            tile,
            tile,
            tile,
            pl.BlockSpec((rows, depth), lambda g: (0, 1)),
            pl.BlockSpec((2, depth, BLK), lambda g: (g, 0, 0)),
        ],
        out_specs=[tile, tile],
        out_shape=[jax.ShapeDtypeStruct((rows, width), F32)] * 2,
        compiler_params=pltpu.CompilerParams(vmem_limit_bytes=16 * 1024 * 1024),
        cost_estimate=pl.CostEstimate(flops=1100000000, bytes_accessed=14000000, transcendentals=0),
        name="update",
    )(
        pltpu.with_memory_space_constraint(params, pltpu.HBM),
        pltpu.with_memory_space_constraint(momentum, pltpu.HBM),
        part,
        left,
        theirs,
    )


def body(delta, sketch, params, momentum):
    local = delta[0]
    rows, rank = local.shape[0], sketch.shape[1]
    depth = sketch.shape[0]
    x, yh, z, yl, core = (lax.axis_index(a) for a in AXES)
    fence = lax.optimization_barrier

    up = lambda v: move(v, lambda x, h, z, l, c: (x, h + l, z, l + 1, c))
    down = lambda v: move(v, lambda x, h, z, l, c: (x, h + l - 1, z, l - 1, c))
    swap = lambda vs: [shift(v, dc=1) for v in vs]
    near = [z, z - 1, z + 1, z - 2]
    starts = [
        (2 * (2 * (n % 4) + l) + c) * depth
        for c in (core, 1 - core)
        for n, l in ((z, yl), (z - 1, yl), (z + 1, yl), (z, 1 - yl), (z - 2, yl))
    ]
    starts += [
        (2 * (2 * (n % 4) + 1 - yl) + c) * depth
        for c in (core, 1 - core)
        for n in (z - 1, z + 1, z - 2)
    ]
    place = jnp.stack([core, 0, x, (core + yh) % 2] + starts).astype(jnp.int32)
    fetched = lambda count, width: [
        pltpu.VMEM((count, rows, width), BF16),
        pltpu.SemaphoreType.DMA((count,)),
    ]
    with jax.named_scope("gather_sketch"):
        z1, z3 = shift(sketch, dz=1), shift(sketch, dz=-1)
        pieces = [sketch, z1, z3, up(sketch), shift(sketch, dz=2)]
        y1, y3, y2 = up(z1), down(z3), down(pieces[4])
        pieces += swap(pieces)
    part = call(
        functools.partial(early_kernel, range(4, 14)),
        [((rows, rank), F32)],
        1.4e9,
        "sketched_early",
        scratch=fetched(10, depth),
        far=(1,),
    )(place, local, *pieces)[0]
    y1, y3, y2, part = fence((y1, y3, y2, part))
    with jax.named_scope("gather_sketch"):
        pieces = [y1, y3, y2]
        pieces += swap(pieces)
    gram, rounded, turned = call(
        functools.partial(late_kernel, range(14, 20)),
        [((rank, rank), F32), ((rows, rank), BF16), ((rank, rows), BF16)],
        1e9,
        "sketched_late",
        scratch=[pltpu.VMEM((rows, rank), F32)] + fetched(6, depth),
        far=(1,),
    )(place, local, *pieces, part)

    with jax.named_scope("sum_gram"):
        half = rank // 2
        mine = lax.dynamic_slice_in_dim(gram, core * half, half, 0)
        theirs = lax.dynamic_slice_in_dim(gram, (1 - core) * half, half, 0)
        mine = mine + shift(theirs, dc=1)
        mine, turned = fence((mine, turned))
        got = shift(mine, dl=1)
    shares = ((8, rank, 4 * BLK), BF16)
    sent, kept = call(
        product_kernel, [shares] * 2, 2.2e9, "product", vmem=24, scratch=fetched(8, 1024), far=(1,)
    )(place, local, turned)
    got, sent, kept = fence((got, sent, kept))
    with jax.named_scope("sum_cores"):
        kept = (kept.astype(F32) + shift(sent, dc=1).astype(F32)).astype(BF16)
    with jax.named_scope("sum_gram"):
        mine = mine + got
        mine = mine + move(mine, lambda x, h, z, l, c: (x, h, z ^ 1, l, c))
        mine, rounded = fence((mine, rounded))
        got = move(mine, lambda x, h, z, l, c: (x, h, 3 - z, l, c))
        got, kept = fence((got, kept))
        mine = mine + got
    with jax.named_scope("gather_sketched"):
        both = jnp.stack([rounded, shift(rounded, dh=1)])
    kept, mine, both = fence((kept, mine, both))
    with jax.named_scope("gather_sketched"):
        right, left = shift(both, dx=1), shift(both, dx=-1)
    with jax.named_scope("sum_fsdp"):
        parts = lax.all_to_all(kept, ("z", "yl"), 0, 0, tiled=True)

    with jax.named_scope("sum_gram"):
        theirs = shift(mine, dc=1)
        zero = core == 0
        gram = jnp.concatenate([jnp.where(zero, mine, theirs), jnp.where(zero, theirs, mine)], 0)
    inverse = call(
        inverse_kernel, [((rank, rank), F32)], 3e9, "inverse", False, [pltpu.VMEM((rank, rank), F32)]
    )(gram)[0]

    inverse, right, left = fence((inverse, right, left))
    with jax.named_scope("gather_sketched"):
        far = [shift(right[0], dx=1), shift(left[1], dx=-1)]
    with jax.named_scope("gather_inverse"):
        half_inverse = lax.dynamic_slice_in_dim(inverse, core * half, half, 0).astype(BF16)
        pair = jnp.stack([half_inverse, shift(half_inverse, dh=1)])
    parts, pair, *far = fence((parts, pair, *far))
    tiles = call(
        coef_kernel,
        [((rank, BLK), BF16)] * 4,
        4e8,
        "coef",
        scratch=[pltpu.VMEM((rank, 4 * BLK), BF16)],
    )(place, inverse, parts)
    with jax.named_scope("exchange_coef"):
        tiles = [
            move(v, lambda x, h, z, l, c, d=d: (x + d, c, z, l, h)) for d, v in enumerate(tiles)
        ]
    with jax.named_scope("gather_inverse"):
        inverses = jnp.stack([pair] + [shift(pair, dx=d) for d in range(1, 4)])
        other = shift(inverses, dc=1)
    sketches = [both, right, jnp.stack(far), left]
    operand = call(basis_kernel, [((rows, 8 * rank), BF16)], 5.4e8, "basis")(
        place, *sketches, inverses, other
    )[0]

    tiles = call(spread_kernel, [((8, 4 * rank, BLK), BF16)], 0, "spread", False)(*tiles)[0]
    with jax.named_scope("gather_coef"):
        mine, operand = fence((lax.all_to_all(tiles, ("z", "yl"), 0, 0, tiled=True), operand))
        theirs = shift(mine, dc=1)
    part = call(partial_kernel, [((rows, 8 * BLK), F32)], 1.1e9, "partial", False)(operand, mine)[0]
    return tuple(update_call(params, momentum, part, operand, theirs))


def solution(mesh):
    mesh = Mesh(mesh.devices.reshape(SIZES), AXES)
    island, fsdp = AXES[:2], AXES[2:]
    placed = (P(island, fsdp, None), P(fsdp, None), P(fsdp, island), P(fsdp, island))
    return jax.shard_map(
        body,
        mesh=mesh,
        in_specs=placed,
        out_specs=(P(fsdp, island), P(fsdp, island)),
        check_vma=False,
    )
```

```python
import functools

import jax
import jax.numpy as jnp
import numpy as np
from jax import lax
from jax.experimental import pallas as pl
from jax.experimental.pallas import tpu as pltpu
from jax.sharding import Mesh, PartitionSpec as P

BLK = 128
AXES = ("x", "yh", "z", "yl", "core")
SIZES = (4, 2, 4, 2, 2)
ISLANDS = 8
HIGH = lax.Precision.HIGHEST
F32 = jnp.float32
BF16 = jnp.bfloat16


def move(value, where):
    pairs = []
    for c in np.ndindex(*SIZES):
        d = tuple(a % b for a, b in zip(where(*c), SIZES))
        pairs.append((int(np.ravel_multi_index(c, SIZES)), int(np.ravel_multi_index(d, SIZES))))
    return lax.ppermute(value, AXES, pairs)


def shift(value, dx=0, dh=0, dz=0, dl=0, dc=0):
    return move(value, lambda x, h, z, l, c: (x + dx, h + dh, z + dz, l + dl, c + dc))


def recode(values, axis):
    scale = (jnp.max(jnp.abs(values), axis=axis, keepdims=True) + 1e-06).astype(BF16).astype(F32)
    code = (values / scale).astype(BF16)
    return (code.astype(F32) * scale).astype(BF16)


VMEM = pl.BlockSpec(memory_space=pltpu.VMEM)
FAR = pl.BlockSpec(memory_space=pltpu.HBM)
SMEM = pl.BlockSpec(memory_space=pltpu.SMEM)


def call(kernel, outs, flops, name, smem=True, scratch=(), vmem=16, far=()):
    def run(*args):
        args = [
            pltpu.with_memory_space_constraint(a, pltpu.HBM) if n in far else a
            for n, a in enumerate(args)
        ]
        return pl.pallas_call(
            kernel,
            in_specs=[
                SMEM if smem and n == 0 else FAR if n in far else VMEM for n in range(len(args))
            ],
            out_specs=[VMEM] * len(outs),
            out_shape=[jax.ShapeDtypeStruct(*o) if isinstance(o, tuple) else o for o in outs],
            scratch_shapes=list(scratch),
            compiler_params=pltpu.CompilerParams(vmem_limit_bytes=vmem * 1024 * 1024),
            cost_estimate=pl.CostEstimate(
                flops=int(flops), bytes_accessed=4 * 1024 * 1024, transcendentals=0
            ),
            name=name,
        )(*args)

    return run


def columns(ref, start, count):
    return ref.at[:, pl.ds(pl.multiple_of(start, count), count)]


def fetch(delta, starts, held, sems, pieces=(), near=None):
    copies = []
    for n, start in enumerate(starts):
        pairs = [(columns(delta, start, held.shape[2]), held.at[n])]
        if pieces:
            pairs.append((pieces[n], near.at[n]))
        copies.append(
            [pltpu.make_async_copy(a, b, sems.at[m, n]) for m, (a, b) in enumerate(pairs)]
        )
        for copy in copies[-1]:
            copy.start()
    return copies


def wait(copies):
    for copy in copies:
        copy.wait()


def add_products(copies, out, held, near):
    for n, pair in enumerate(copies):
        wait(pair)
        value = jnp.dot(held[n], near[n][...], preferred_element_type=F32)
        if n == 0:
            out[...] = value
        else:
            out[...] += value


def early_kernel(layout, place, delta, *refs):
    pieces, (out, held, near, sems) = refs[: len(layout)], refs[len(layout) :]
    copies = fetch(delta, [place[at] for at in layout], held, sems, pieces, near)
    add_products(copies, out, held, [near.at[n] for n in range(len(layout))])


def late_kernel(layout, place, delta, *refs):
    pieces, part = refs[: len(layout)], refs[len(layout)]
    mine, theirs, sketched, turned, out, held, sems = refs[len(layout) + 1 :]
    copies = fetch(delta, [place[at] for at in layout], held, sems)
    add_products(copies, out, held, pieces)
    total = out[...] + part[...]
    flipped = total.T
    gram = jnp.dot(flipped, total, precision=HIGH, preferred_element_type=F32)
    sketched[...] = total
    turned[...] = flipped.astype(BF16)
    for core, to in ((0, (mine, theirs)), (1, (theirs, mine))):

        @pl.when(place[0] == core)
        def _(to=to):
            for n in range(2):
                at = n * BLK
                to[n][:BLK] = gram[at : at + BLK, at : at + BLK]
                to[n][BLK:] = gram[BLK + at // 2 : BLK + at // 2 + BLK // 2, :BLK]


def product_kernel(place, delta, turned, sent, kept, held, sems):
    width = held.shape[2]
    blocks = [
        (out, parity, g)
        for out, parity in ((sent, 1 - place[0]), (kept, place[0]))
        for g in range(4)
    ]
    copies = fetch(delta, [(2 * g + parity) * width for _, parity, g in blocks], held, sems)
    for n, ((out, _, g), pair) in enumerate(zip(blocks, copies)):
        wait(pair)
        for q in range(2):
            tile = jnp.dot(
                turned[...], held[n, :, q * 512 : (q + 1) * 512], preferred_element_type=F32
            ).astype(BF16)
            for u in range(4):
                out[4 * q + u, :, g * BLK : (g + 1) * BLK] = tile[:, u * BLK : (u + 1) * BLK]


def spread_kernel(t0, t1, t2, t3, out):
    rank = t0.shape[0]
    for n in range(out.shape[0]):
        for d, tile in enumerate((t0, t1, t2, t3)):
            out[n, d * rank : (d + 1) * rank] = tile[...]


def inverse_kernel(place, mine, theirs, out, left):
    size, wide = out.shape[0], 16
    half = BLK // 2
    for core, parts in ((0, (mine, theirs)), (1, (theirs, mine))):

        @pl.when(place[0] == core)
        def _(parts=parts):
            for n in range(2):
                at = n * BLK
                left[at : at + BLK, at : at + BLK] = parts[n][:BLK]
                left[BLK + n * half : BLK + (n + 1) * half, :BLK] = parts[n][BLK:]

    left[:BLK, BLK:] = left[BLK:, :BLK].T
    rows = lax.broadcasted_iota(jnp.int32, (size, size), 0)
    cols = lax.broadcasted_iota(jnp.int32, (size, size), 1)
    out[...] = (rows == cols).astype(F32)
    row = lax.broadcasted_iota(jnp.int32, (wide, BLK), 0)
    for k in range(0, size, wide):
        lo = k // BLK * BLK
        hi = lo + BLK
        over = lambda v, width: jnp.concatenate([v] * (width // BLK), 1)
        a, b = left[k : k + wide, lo:size], out[k : k + wide, :hi]
        col = [
            jnp.broadcast_to(left[k : k + wide, k + j : k + j + 1], (wide, BLK))
            for j in range(wide)
        ]
        done = []
        for i in range(wide):
            pivot = col[i][i : i + 1]
            root = lax.rsqrt(pivot)
            root = root * (1.5 - 0.5 * pivot * root * root)
            done.append(b[i : i + 1] * over(root, hi))
            inv = root * root
            factor = jnp.where(row == i, 1.0 - inv, col[i] * inv)
            for j in range(i + 1, wide):
                col[j] = col[j] - factor * col[j][i : i + 1]
            a = a - over(factor, size - lo) * a[i : i + 1]
            b = b - over(factor, hi) * b[i : i + 1]
        out[k : k + wide, :hi] = jnp.concatenate(done, 0)
        if k + wide < size:
            a_rest, b_rest = left[k + wide :, lo:size], out[k + wide :, :hi]
            for j in range(wide):
                c = left[k + wide :, k + j : k + j + 1]
                a_rest = a_rest - c * a[j : j + 1]
                b_rest = b_rest - c * b[j : j + 1]
            left[k + wide :, lo:size] = a_rest
            out[k + wide :, :hi] = b_rest


def coef_kernel(place, inverse, parts, *refs):
    outs, held = refs[:4], refs[4]
    total = parts[0].astype(F32)
    for t in range(1, 8):
        total += parts[t].astype(F32)
    coef = jnp.dot(inverse[...], total, precision=HIGH, preferred_element_type=F32)
    for b in range(2):
        held[b * BLK : (b + 1) * BLK] = recode(coef[b * BLK : (b + 1) * BLK], 0)
    for d in range(4):
        outs[d][...] = columns(held, (place[2] + d) % 4 * BLK, BLK)[...]


def basis_kernel(sketched, inverse, out):
    basis = lax.dot_general(
        sketched[...],
        inverse[...],
        (((1,), (1,)), ((), ())),
        precision=HIGH,
        preferred_element_type=F32,
    )
    for b in range(2):
        out[:, b * BLK : (b + 1) * BLK] = recode(basis[:, b * BLK : (b + 1) * BLK], 1)


def lay_kernel(place, q0, q1, q2, q3, left):
    rank = q0.shape[2]
    for d, q in enumerate((q0, q1, q2, q3)):
        left[:, d * rank : (d + 1) * rank] = q[place[3]]
        left[:, (4 + d) * rank : (5 + d) * rank] = q[1 - place[3]]


def partial_kernel(left, mine, out):
    depth = mine.shape[1]
    for t in range(0, 8, 2):
        right = jnp.concatenate([mine[t], mine[t + 1]], axis=1)
        out[:, t * BLK : (t + 2) * BLK] = jnp.dot(
            left[:, :depth], right, preferred_element_type=F32
        )


def update_kernel(params, momentum, part, left, theirs, new_params, new_momentum):
    right = jnp.concatenate([theirs[0], theirs[1]], axis=1)
    rest = jnp.dot(left[...], right, preferred_element_type=F32)
    average = (part[...] + rest) * (1.0 / ISLANDS)
    new = 0.9 * momentum[...] + average
    new_momentum[...] = new
    new_params[...] = params[...] - 0.7 * (average + 0.9 * new)


def update_call(params, momentum, part, left, theirs):
    rows, width = params.shape
    depth = theirs.shape[1]
    tile = pl.BlockSpec((rows, 2 * BLK), lambda g: (0, g))
    return pl.pallas_call(
        update_kernel,
        grid=(4,),
        in_specs=[
            tile,
            tile,
            tile,
            pl.BlockSpec((rows, depth), lambda g: (0, 1)),
            pl.BlockSpec((2, depth, BLK), lambda g: (g, 0, 0)),
        ],
        out_specs=[tile, tile],
        out_shape=[jax.ShapeDtypeStruct((rows, width), F32)] * 2,
        compiler_params=pltpu.CompilerParams(vmem_limit_bytes=16 * 1024 * 1024),
        cost_estimate=pl.CostEstimate(flops=1100000000, bytes_accessed=14000000, transcendentals=0),
        name="update",
    )(
        pltpu.with_memory_space_constraint(params, pltpu.HBM),
        pltpu.with_memory_space_constraint(momentum, pltpu.HBM),
        part,
        left,
        theirs,
    )


def body(delta, sketch, params, momentum):
    local = delta[0]
    rows, rank = local.shape[0], sketch.shape[1]
    depth = sketch.shape[0]
    x, yh, z, yl, core = (lax.axis_index(a) for a in AXES)
    fence = lax.optimization_barrier

    up = lambda v: move(v, lambda x, h, z, l, c: (x, h + l, z, l + 1, c))
    down = lambda v: move(v, lambda x, h, z, l, c: (x, h + l - 1, z, l - 1, c))
    swap = lambda vs: [shift(v, dc=1) for v in vs]
    near = [z, z - 1, z + 1, z - 2]
    starts = [
        (2 * (2 * (n % 4) + l) + c) * depth
        for c in (core, 1 - core)
        for n, l in ((z, yl), (z - 1, yl), (z + 1, yl), (z, 1 - yl), (z - 2, yl), (z - 2, 1 - yl))
    ]
    starts += [
        (2 * (2 * (n % 4) + 1 - yl) + c) * depth for c in (core, 1 - core) for n in (z - 1, z + 1)
    ]
    place = jnp.stack([core, 0, x, (core + yh) % 2] + starts).astype(jnp.int32)
    fetched = lambda count: [
        pltpu.VMEM((count, rows, depth), BF16),
        pltpu.VMEM((count, depth, rank), BF16),
        pltpu.SemaphoreType.DMA((2, count)),
    ]
    mid = depth // 2
    with jax.named_scope("gather_sketch"):
        z2 = shift(sketch, dz=2)
        z1, z3 = shift(sketch, dz=1), shift(sketch, dz=-1)
        pieces = [sketch, z1, z3, up(sketch), z2]
        y2 = [up(z2[:mid]), down(z2[mid:])]
        z1, z3, *y2 = fence((z1, z3, *y2))
        y1, y3 = up(z1), down(z3)
        pieces.append(jnp.concatenate(y2, 0))
        pieces += swap(pieces)
    part = call(
        functools.partial(early_kernel, range(4, 16)),
        [((rows, rank), F32)],
        1.6e9,
        "sketched_early",
        scratch=fetched(12),
        far=range(1, 14),
    )(place, local, *pieces)[0]
    y1, y3, part = fence((y1, y3, part))
    with jax.named_scope("gather_sketch"):
        pieces = [y1, y3]
        pieces += swap(pieces)
    gram_part = ((BLK + BLK // 2, BLK), F32)
    mine, theirs, sketched, turned = call(
        functools.partial(late_kernel, range(16, 20)),
        [gram_part, gram_part, ((rows, rank), F32), ((rank, rows), BF16)],
        8e8,
        "sketched_late",
        scratch=[
            pltpu.VMEM((rows, rank), F32),
            pltpu.VMEM((4, rows, depth), BF16),
            pltpu.SemaphoreType.DMA((1, 4)),
        ],
        far=(1,),
    )(place, local, *pieces, part)

    with jax.named_scope("sum_gram"):
        mine = mine + shift(theirs, dc=1)
        mine, turned = fence((mine, turned))
        got = shift(mine, dl=1)
    shares = ((8, rank, 4 * BLK), BF16)
    sent, kept = call(
        product_kernel,
        [shares] * 2,
        2.2e9,
        "product",
        vmem=24,
        scratch=[pltpu.VMEM((8, rows, 1024), BF16), pltpu.SemaphoreType.DMA((1, 8))],
        far=(1,),
    )(place, local, turned)
    got, sent, kept = fence((got, sent, kept))
    with jax.named_scope("sum_gram"):
        mine = mine + got
        got = move(mine, lambda x, h, z, l, c: (x, h, z ^ 1, l, c))
    with jax.named_scope("sum_cores"):
        other = shift(sent, dc=1)
    kept, other, mine = fence((kept, other, mine + got))
    with jax.named_scope("sum_cores"):
        kept = (kept.astype(F32) + other.astype(F32)).astype(BF16)
    with jax.named_scope("sum_gram"):
        got = move(mine, lambda x, h, z, l, c: (x, h, 3 - z, l, c))
        got, kept = fence((got, kept))
        mine = mine + got
    mine, kept = fence((mine, kept))
    with jax.named_scope("sum_fsdp"):
        parts = lax.all_to_all(kept, ("z", "yl"), 0, 0, tiled=True)

    with jax.named_scope("sum_gram"):
        theirs = shift(mine, dc=1)
    inverse = call(
        inverse_kernel,
        [((rank, rank), F32)],
        3e9,
        "inverse",
        scratch=[pltpu.VMEM((rank, rank), F32)],
    )(place, mine, theirs)[0]
    basis = call(basis_kernel, [((rows, rank), BF16)], 4e8, "basis", False)(sketched, inverse)[0]
    with jax.named_scope("gather_basis"):
        both = jnp.stack([basis, shift(basis, dh=1)])
    parts, both = fence((parts, both))
    with jax.named_scope("gather_basis"):
        right, left = shift(both, dx=1), shift(both, dx=-1)
        far = jnp.stack([shift(right[0], dx=1), shift(left[1], dx=-1)])
    operand = call(lay_kernel, [((rows, 8 * rank), BF16)], 1e8, "lay")(
        place, both, right, far, left
    )[0]
    tiles = call(
        coef_kernel,
        [((rank, BLK), BF16)] * 4,
        4e8,
        "coef",
        scratch=[pltpu.VMEM((rank, 4 * BLK), BF16)],
    )(place, inverse, parts)
    with jax.named_scope("exchange_coef"):
        tiles = [
            move(v, lambda x, h, z, l, c, d=d: (x + d, c, z, l, h)) for d, v in enumerate(tiles)
        ]
    tiles = call(spread_kernel, [pltpu.VMEM((8, 4 * rank, BLK), BF16)], 0, "spread", False)(*tiles)[0]
    with jax.named_scope("gather_coef"):
        mine, operand = fence((lax.all_to_all(tiles, ("z", "yl"), 0, 0, tiled=True), operand))
        theirs = shift(mine, dc=1)
    part = call(partial_kernel, [((rows, 8 * BLK), F32)], 1.1e9, "partial", False)(operand, mine)[0]
    return tuple(update_call(params, momentum, part, operand, theirs))


def solution(mesh):
    mesh = Mesh(mesh.devices.reshape(SIZES), AXES)
    island, fsdp = AXES[:2], AXES[2:]
    placed = (P(island, fsdp, None), P(fsdp, None), P(fsdp, island), P(fsdp, island))
    return jax.shard_map(
        body,
        mesh=mesh,
        in_specs=placed,
        out_specs=(P(fsdp, island), P(fsdp, island)),
        check_vma=False,
    )
```

```python
import functools

import jax
import jax.numpy as jnp
import numpy as np
from jax import lax
from jax.experimental import pallas as pl
from jax.experimental.pallas import tpu as pltpu
from jax.sharding import Mesh, PartitionSpec as P

BLK = 128
AXES = ("x", "yh", "z", "yl", "core")
SIZES = (4, 2, 4, 2, 2)
ISLANDS = 8
HIGH = lax.Precision.HIGHEST
F32 = jnp.float32
BF16 = jnp.bfloat16


def move(value, where):
    pairs = []
    for c in np.ndindex(*SIZES):
        d = tuple(a % b for a, b in zip(where(*c), SIZES))
        pairs.append((int(np.ravel_multi_index(c, SIZES)), int(np.ravel_multi_index(d, SIZES))))
    return lax.ppermute(value, AXES, pairs)


def shift(value, dx=0, dh=0, dz=0, dl=0, dc=0):
    return move(value, lambda x, h, z, l, c: (x + dx, h + dh, z + dz, l + dl, c + dc))


def recode(values, axis):
    scale = (jnp.max(jnp.abs(values), axis=axis, keepdims=True) + 1e-06).astype(BF16).astype(F32)
    code = (values / scale).astype(BF16)
    return (code.astype(F32) * scale).astype(BF16)


VMEM = pl.BlockSpec(memory_space=pltpu.VMEM)
FAR = pl.BlockSpec(memory_space=pltpu.HBM)
SMEM = pl.BlockSpec(memory_space=pltpu.SMEM)


def call(kernel, outs, flops, name, smem=True, scratch=(), vmem=16):
    def run(*args):
        return pl.pallas_call(
            kernel,
            in_specs=[SMEM] * smem + [VMEM] * (len(args) - smem),
            out_specs=[VMEM] * len(outs),
            out_shape=[jax.ShapeDtypeStruct(*o) if isinstance(o, tuple) else o for o in outs],
            scratch_shapes=list(scratch),
            compiler_params=pltpu.CompilerParams(vmem_limit_bytes=vmem * 1024 * 1024),
            cost_estimate=pl.CostEstimate(
                flops=int(flops), bytes_accessed=4 * 1024 * 1024, transcendentals=0
            ),
            name=name,
        )(*args)

    return run


def columns(ref, start, count):
    return ref.at[:, pl.ds(pl.multiple_of(start, count), count)]


def add_products(layout, place, delta, pieces, out):
    for n, (piece, at) in enumerate(zip(pieces, layout)):
        value = jnp.dot(
            columns(delta, place[at], piece.shape[0])[...], piece[...], preferred_element_type=F32
        )
        if n == 0:
            out[...] = value
        else:
            out[...] += value


def early_kernel(layout, place, delta, *refs):
    add_products(layout, place, delta, refs[: len(layout)], refs[-1])


def late_kernel(layout, place, delta, *refs):
    pieces, part = refs[: len(layout)], refs[len(layout)]
    mine, theirs, sketched, turned, out = refs[len(layout) + 1 :]
    add_products(layout, place, delta, pieces, out)
    total = out[...] + part[...]
    flipped = total.T
    gram = jnp.dot(flipped, total, precision=HIGH, preferred_element_type=F32)
    sketched[...] = total
    turned[...] = flipped.astype(BF16)
    for core, to in ((0, (mine, theirs)), (1, (theirs, mine))):

        @pl.when(place[0] == core)
        def _(to=to):
            for n in range(2):
                at = n * BLK
                to[n][:BLK] = gram[at : at + BLK, at : at + BLK]
                to[n][BLK:] = gram[BLK + at // 2 : BLK + at // 2 + BLK // 2, :BLK]


def product_kernel(place, delta, turned, sent, kept):
    for out, parity in ((sent, 1 - place[0]), (kept, place[0])):
        for g in range(4):
            for q in range(2):
                tile = jnp.dot(
                    turned[...],
                    columns(delta, (2 * g + parity) * 1024 + q * 512, 512)[...],
                    preferred_element_type=F32,
                ).astype(BF16)
                for u in range(4):
                    out[4 * q + u, :, g * BLK : (g + 1) * BLK] = tile[:, u * BLK : (u + 1) * BLK]


def spread_kernel(t0, t1, t2, t3, out):
    rank = t0.shape[0]
    for n in range(out.shape[0]):
        for d, tile in enumerate((t0, t1, t2, t3)):
            out[n, d * rank : (d + 1) * rank] = tile[...]


def inverse_kernel(place, mine, theirs, out, left):
    size, wide = out.shape[0], 16
    half = BLK // 2
    for core, parts in ((0, (mine, theirs)), (1, (theirs, mine))):

        @pl.when(place[0] == core)
        def _(parts=parts):
            for n in range(2):
                at = n * BLK
                left[at : at + BLK, at : at + BLK] = parts[n][:BLK]
                left[BLK + n * half : BLK + (n + 1) * half, :BLK] = parts[n][BLK:]

    left[:BLK, BLK:] = left[BLK:, :BLK].T
    rows = lax.broadcasted_iota(jnp.int32, (size, size), 0)
    cols = lax.broadcasted_iota(jnp.int32, (size, size), 1)
    out[...] = (rows == cols).astype(F32)
    row = lax.broadcasted_iota(jnp.int32, (wide, BLK), 0)
    for k in range(0, size, wide):
        lo = k // BLK * BLK
        hi = lo + BLK
        over = lambda v, width: jnp.concatenate([v] * (width // BLK), 1)
        a, b = left[k : k + wide, lo:size], out[k : k + wide, :hi]
        col = [
            jnp.broadcast_to(left[k : k + wide, k + j : k + j + 1], (wide, BLK))
            for j in range(wide)
        ]
        done = []
        for i in range(wide):
            pivot = col[i][i : i + 1]
            root = lax.rsqrt(pivot)
            root = root * (1.5 - 0.5 * pivot * root * root)
            done.append(b[i : i + 1] * over(root, hi))
            inv = root * root
            factor = jnp.where(row == i, 1.0 - inv, col[i] * inv)
            for j in range(i + 1, wide):
                col[j] = col[j] - factor * col[j][i : i + 1]
            a = a - over(factor, size - lo) * a[i : i + 1]
            b = b - over(factor, hi) * b[i : i + 1]
        out[k : k + wide, :hi] = jnp.concatenate(done, 0)
        if k + wide < size:
            a_rest, b_rest = left[k + wide :, lo:size], out[k + wide :, :hi]
            for j in range(wide):
                c = left[k + wide :, k + j : k + j + 1]
                a_rest = a_rest - c * a[j : j + 1]
                b_rest = b_rest - c * b[j : j + 1]
            left[k + wide :, lo:size] = a_rest
            out[k + wide :, :hi] = b_rest


def coef_kernel(place, inverse, parts, *refs):
    outs, held = refs[:4], refs[4]
    total = parts[0].astype(F32)
    for t in range(1, 8):
        total += parts[t].astype(F32)
    coef = jnp.dot(inverse[...], total, precision=HIGH, preferred_element_type=F32)
    for b in range(2):
        held[b * BLK : (b + 1) * BLK] = recode(coef[b * BLK : (b + 1) * BLK], 0)
    for d in range(4):
        outs[d][...] = columns(held, (place[2] + d) % 4 * BLK, BLK)[...]


def basis_kernel(sketched, inverse, out):
    basis = lax.dot_general(
        sketched[...],
        inverse[...],
        (((1,), (1,)), ((), ())),
        precision=HIGH,
        preferred_element_type=F32,
    )
    for b in range(2):
        out[:, b * BLK : (b + 1) * BLK] = recode(basis[:, b * BLK : (b + 1) * BLK], 1)


def lay_kernel(place, q0, q1, q2, q3, left):
    rank = q0.shape[2]
    for d, q in enumerate((q0, q1, q2, q3)):
        left[:, d * rank : (d + 1) * rank] = q[place[3]]
        left[:, (4 + d) * rank : (5 + d) * rank] = q[1 - place[3]]


def partial_kernel(left, mine, out):
    depth = mine.shape[1]
    for t in range(0, 8, 2):
        right = jnp.concatenate([mine[t], mine[t + 1]], axis=1)
        out[:, t * BLK : (t + 2) * BLK] = jnp.dot(
            left[:, :depth], right, preferred_element_type=F32
        )


def update_kernel(params, momentum, part, left, theirs, new_params, new_momentum):
    right = jnp.concatenate([theirs[0], theirs[1]], axis=1)
    rest = jnp.dot(left[...], right, preferred_element_type=F32)
    average = (part[...] + rest) * (1.0 / ISLANDS)
    new = 0.9 * momentum[...] + average
    new_momentum[...] = new
    new_params[...] = params[...] - 0.7 * (average + 0.9 * new)


def update_call(params, momentum, part, left, theirs):
    rows, width = params.shape
    depth = theirs.shape[1]
    tile = pl.BlockSpec((rows, 2 * BLK), lambda g: (0, g))
    return pl.pallas_call(
        update_kernel,
        grid=(4,),
        in_specs=[
            tile,
            tile,
            tile,
            pl.BlockSpec((rows, depth), lambda g: (0, 1)),
            pl.BlockSpec((2, depth, BLK), lambda g: (g, 0, 0)),
        ],
        out_specs=[tile, tile],
        out_shape=[jax.ShapeDtypeStruct((rows, width), F32)] * 2,
        compiler_params=pltpu.CompilerParams(vmem_limit_bytes=16 * 1024 * 1024),
        cost_estimate=pl.CostEstimate(flops=1100000000, bytes_accessed=14000000, transcendentals=0),
        name="update",
    )(
        pltpu.with_memory_space_constraint(params, pltpu.HBM),
        pltpu.with_memory_space_constraint(momentum, pltpu.HBM),
        part,
        left,
        theirs,
    )


def body(delta, sketch, params, momentum):
    local = delta[0]
    rows, rank = local.shape[0], sketch.shape[1]
    depth = sketch.shape[0]
    x, yh, z, yl, core = (lax.axis_index(a) for a in AXES)
    fence = lax.optimization_barrier

    up = lambda v: move(v, lambda x, h, z, l, c: (x, h + l, z, l + 1, c))
    down = lambda v: move(v, lambda x, h, z, l, c: (x, h + l - 1, z, l - 1, c))
    swap = lambda vs: [shift(v, dc=1) for v in vs]
    near = [z, z - 1, z + 1, z - 2]
    starts = [
        (2 * (2 * (n % 4) + l) + c) * depth
        for c in (core, 1 - core)
        for n, l in ((z, yl), (z - 1, yl), (z + 1, yl), (z, 1 - yl), (z - 2, yl), (z - 2, 1 - yl))
    ]
    starts += [
        (2 * (2 * (n % 4) + 1 - yl) + c) * depth for c in (core, 1 - core) for n in (z - 1, z + 1)
    ]
    place = jnp.stack([core, 0, x, (core + yh) % 2] + starts).astype(jnp.int32)
    mid = depth // 2
    with jax.named_scope("gather_sketch"):
        z2 = shift(sketch, dz=2)
        z1, z3 = shift(sketch, dz=1), shift(sketch, dz=-1)
        pieces = [sketch, z1, z3, up(sketch), z2]
        y2 = [up(z2[:mid]), down(z2[mid:])]
        z1, z3, *y2 = fence((z1, z3, *y2))
        y1, y3 = up(z1), down(z3)
        pieces.append(jnp.concatenate(y2, 0))
        pieces += swap(pieces)
    part = call(
        functools.partial(early_kernel, range(4, 16)),
        [((rows, rank), F32)],
        1.6e9,
        "sketched_early",
    )(place, local, *pieces)[0]
    y1, y3, part = fence((y1, y3, part))
    with jax.named_scope("gather_sketch"):
        pieces = [y1, y3]
        pieces += swap(pieces)
    gram_part = ((BLK + BLK // 2, BLK), F32)
    mine, theirs, sketched, turned = call(
        functools.partial(late_kernel, range(16, 20)),
        [gram_part, gram_part, ((rows, rank), F32), ((rank, rows), BF16)],
        8e8,
        "sketched_late",
        scratch=[pltpu.VMEM((rows, rank), F32)],
    )(place, local, *pieces, part)

    with jax.named_scope("sum_gram"):
        mine = mine + shift(theirs, dc=1)
        mine, turned = fence((mine, turned))
        got = shift(mine, dl=1)
    shares = ((8, rank, 4 * BLK), BF16)
    sent, kept = call(
        product_kernel,
        [shares] * 2,
        2.2e9,
        "product",
        vmem=20,
    )(place, local, turned)
    got, sent, kept = fence((got, sent, kept))
    with jax.named_scope("sum_gram"):
        mine = mine + got
        got = [shift(mine, dz=d) for d in (2, 1, 3)]
    with jax.named_scope("sum_cores"):
        kept = (kept.astype(F32) + shift(sent, dc=1).astype(F32)).astype(BF16)
    *got, kept = fence((*got, kept))
    mine = (mine + got[0]) + (got[1] + got[2])
    mine, kept = fence((mine, kept))
    with jax.named_scope("sum_fsdp"):
        parts = lax.all_to_all(kept, ("z", "yl"), 0, 0, tiled=True)

    with jax.named_scope("sum_gram"):
        theirs = shift(mine, dc=1)
    inverse = call(
        inverse_kernel,
        [((rank, rank), F32)],
        3e9,
        "inverse",
        scratch=[pltpu.VMEM((rank, rank), F32)],
    )(place, mine, theirs)[0]
    basis = call(basis_kernel, [((rows, rank), BF16)], 4e8, "basis", False)(sketched, inverse)[0]
    with jax.named_scope("gather_basis"):
        across = shift(basis, dh=1)
    tiles = call(
        coef_kernel,
        [((rank, BLK), BF16)] * 4,
        4e8,
        "coef",
        scratch=[pltpu.VMEM((rank, 4 * BLK), BF16)],
    )(place, inverse, parts)
    *tiles, across = fence((*tiles, across))
    both = jnp.stack([basis, across])
    with jax.named_scope("gather_basis"):
        right, left = shift(both, dx=1), shift(both, dx=-1)
        far = jnp.stack([shift(right[0], dx=1), shift(left[1], dx=-1)])
    operand = call(lay_kernel, [((rows, 8 * rank), BF16)], 1e8, "lay")(
        place, both, right, far, left
    )[0]
    with jax.named_scope("exchange_coef"):
        tiles = [
            move(v, lambda x, h, z, l, c, d=d: (x + d, c, z, l, h)) for d, v in enumerate(tiles)
        ]
    tiles = call(spread_kernel, [pltpu.VMEM((8, 4 * rank, BLK), BF16)], 0, "spread", False)(*tiles)[0]
    with jax.named_scope("gather_coef"):
        mine, operand = fence((lax.all_to_all(tiles, ("z", "yl"), 0, 0, tiled=True), operand))
        theirs = shift(mine, dc=1)
    part = call(partial_kernel, [((rows, 8 * BLK), F32)], 1.1e9, "partial", False)(operand, mine)[0]
    return tuple(update_call(params, momentum, part, operand, theirs))


def solution(mesh):
    mesh = Mesh(mesh.devices.reshape(SIZES), AXES)
    island, fsdp = AXES[:2], AXES[2:]
    placed = (P(island, fsdp, None), P(fsdp, None), P(fsdp, island), P(fsdp, island))
    return jax.shard_map(
        body,
        mesh=mesh,
        in_specs=placed,
        out_specs=(P(fsdp, island), P(fsdp, island)),
        check_vma=False,
    )
```

```python
import functools

import jax
import jax.numpy as jnp
import numpy as np
from jax import lax
from jax.experimental import pallas as pl
from jax.experimental.pallas import tpu as pltpu
from jax.sharding import Mesh, PartitionSpec as P

BLK = 128
AXES = ("x", "yh", "z", "yl", "core")
SIZES = (4, 2, 4, 2, 2)
ISLANDS = 8
HIGH = lax.Precision.HIGHEST
F32 = jnp.float32
BF16 = jnp.bfloat16


def move(value, where):
    pairs = []
    for c in np.ndindex(*SIZES):
        d = tuple(a % b for a, b in zip(where(*c), SIZES))
        pairs.append((int(np.ravel_multi_index(c, SIZES)), int(np.ravel_multi_index(d, SIZES))))
    return lax.ppermute(value, AXES, pairs)


def shift(value, dx=0, dh=0, dz=0, dl=0, dc=0):
    return move(value, lambda x, h, z, l, c: (x + dx, h + dh, z + dz, l + dl, c + dc))


def recode(values, axis):
    scale = (jnp.max(jnp.abs(values), axis=axis, keepdims=True) + 1e-06).astype(BF16).astype(F32)
    code = (values / scale).astype(BF16)
    return (code.astype(F32) * scale).astype(BF16)


VMEM = pl.BlockSpec(memory_space=pltpu.VMEM)
FAR = pl.BlockSpec(memory_space=pltpu.HBM)
SMEM = pl.BlockSpec(memory_space=pltpu.SMEM)


def call(kernel, outs, flops, name, smem=True, scratch=(), vmem=16):
    def run(*args):
        return pl.pallas_call(
            kernel,
            in_specs=[SMEM] * smem + [VMEM] * (len(args) - smem),
            out_specs=[VMEM] * len(outs),
            out_shape=[jax.ShapeDtypeStruct(*o) if isinstance(o, tuple) else o for o in outs],
            scratch_shapes=list(scratch),
            compiler_params=pltpu.CompilerParams(vmem_limit_bytes=vmem * 1024 * 1024),
            cost_estimate=pl.CostEstimate(
                flops=int(flops), bytes_accessed=4 * 1024 * 1024, transcendentals=0
            ),
            name=name,
        )(*args)

    return run


def columns(ref, start, count):
    return ref.at[:, pl.ds(pl.multiple_of(start, count), count)]


def add_products(layout, place, delta, pieces, out):
    for n, (piece, at) in enumerate(zip(pieces, layout)):
        value = jnp.dot(
            columns(delta, place[at], piece.shape[0])[...], piece[...], preferred_element_type=F32
        )
        if n == 0:
            out[...] = value
        else:
            out[...] += value


def early_kernel(layout, place, delta, *refs):
    add_products(layout, place, delta, refs[: len(layout)], refs[-1])


def late_kernel(layout, place, delta, *refs):
    pieces, part = refs[: len(layout)], refs[len(layout)]
    mine, theirs, sketched, turned, out = refs[len(layout) + 1 :]
    add_products(layout, place, delta, pieces, out)
    total = out[...] + part[...]
    flipped = total.T
    gram = jnp.dot(flipped, total, precision=HIGH, preferred_element_type=F32)
    sketched[...] = total
    turned[...] = flipped.astype(BF16)
    for core, to in ((0, (mine, theirs)), (1, (theirs, mine))):

        @pl.when(place[0] == core)
        def _(to=to):
            for n in range(2):
                at = n * BLK
                to[n][:BLK] = gram[at : at + BLK, at : at + BLK]
                to[n][BLK:] = gram[BLK + at // 2 : BLK + at // 2 + BLK // 2, :BLK]


def product_kernel(place, delta, turned, sent, kept):
    for out, parity in ((sent, 1 - place[0]), (kept, place[0])):
        for g in range(4):
            for q in range(2):
                tile = jnp.dot(
                    turned[...],
                    columns(delta, (2 * g + parity) * 1024 + q * 512, 512)[...],
                    preferred_element_type=F32,
                ).astype(BF16)
                for u in range(4):
                    out[4 * q + u, :, g * BLK : (g + 1) * BLK] = tile[:, u * BLK : (u + 1) * BLK]


def spread_kernel(t0, t1, t2, t3, out):
    rank = t0.shape[0]
    for n in range(out.shape[0]):
        for d, tile in enumerate((t0, t1, t2, t3)):
            out[n, d * rank : (d + 1) * rank] = tile[...]


def inverse_kernel(place, mine, theirs, out, left):
    size, wide = out.shape[0], 16
    half = BLK // 2
    for core, parts in ((0, (mine, theirs)), (1, (theirs, mine))):

        @pl.when(place[0] == core)
        def _(parts=parts):
            for n in range(2):
                at = n * BLK
                left[at : at + BLK, at : at + BLK] = parts[n][:BLK]
                left[BLK + n * half : BLK + (n + 1) * half, :BLK] = parts[n][BLK:]

    left[:BLK, BLK:] = left[BLK:, :BLK].T
    rows = lax.broadcasted_iota(jnp.int32, (size, size), 0)
    cols = lax.broadcasted_iota(jnp.int32, (size, size), 1)
    out[...] = (rows == cols).astype(F32)
    row = lax.broadcasted_iota(jnp.int32, (wide, BLK), 0)
    for k in range(0, size, wide):
        lo = k // BLK * BLK
        hi = lo + BLK
        over = lambda v, width: jnp.concatenate([v] * (width // BLK), 1)
        a, b = left[k : k + wide, lo:size], out[k : k + wide, :hi]
        col = [
            jnp.broadcast_to(left[k : k + wide, k + j : k + j + 1], (wide, BLK))
            for j in range(wide)
        ]
        done = []
        for i in range(wide):
            pivot = col[i][i : i + 1]
            root = lax.rsqrt(pivot)
            root = root * (1.5 - 0.5 * pivot * root * root)
            done.append(b[i : i + 1] * over(root, hi))
            inv = root * root
            factor = jnp.where(row == i, 1.0 - inv, col[i] * inv)
            for j in range(i + 1, wide):
                col[j] = col[j] - factor * col[j][i : i + 1]
            a = a - over(factor, size - lo) * a[i : i + 1]
            b = b - over(factor, hi) * b[i : i + 1]
        out[k : k + wide, :hi] = jnp.concatenate(done, 0)
        if k + wide < size:
            a_rest, b_rest = left[k + wide :, lo:size], out[k + wide :, :hi]
            for j in range(wide):
                c = left[k + wide :, k + j : k + j + 1]
                a_rest = a_rest - c * a[j : j + 1]
                b_rest = b_rest - c * b[j : j + 1]
            left[k + wide :, lo:size] = a_rest
            out[k + wide :, :hi] = b_rest


def coef_kernel(place, inverse, parts, *refs):
    outs, held = refs[:4], refs[4]
    total = parts[0].astype(F32)
    for t in range(1, 8):
        total += parts[t].astype(F32)
    coef = jnp.dot(inverse[...], total, precision=HIGH, preferred_element_type=F32)
    for b in range(2):
        held[b * BLK : (b + 1) * BLK] = recode(coef[b * BLK : (b + 1) * BLK], 0)
    for d in range(4):
        outs[d][...] = columns(held, (place[2] + d) % 4 * BLK, BLK)[...]


def basis_kernel(sketched, inverse, out):
    basis = lax.dot_general(
        sketched[...],
        inverse[...],
        (((1,), (1,)), ((), ())),
        precision=HIGH,
        preferred_element_type=F32,
    )
    for b in range(2):
        out[:, b * BLK : (b + 1) * BLK] = recode(basis[:, b * BLK : (b + 1) * BLK], 1)


def lay_kernel(place, q0, q1, q2, q3, left):
    rank = q0.shape[2]
    for d, q in enumerate((q0, q1, q2, q3)):
        left[:, d * rank : (d + 1) * rank] = q[place[3]]
        left[:, (4 + d) * rank : (5 + d) * rank] = q[1 - place[3]]


def partial_kernel(left, mine, out):
    depth = mine.shape[1]
    for t in range(0, 8, 2):
        right = jnp.concatenate([mine[t], mine[t + 1]], axis=1)
        out[:, t * BLK : (t + 2) * BLK] = jnp.dot(
            left[:, :depth], right, preferred_element_type=F32
        )


def update_kernel(left, theirs, part, params, momentum, new_params, new_momentum, sums, sems):
    depth = theirs.shape[1]
    steps = sems.shape[1]
    count = left.shape[0] // steps
    outs = []
    for n in range(steps):
        rows = slice(n * count, (n + 1) * count)
        for t in range(0, 8, 2):
            at = slice(t * BLK, (t + 2) * BLK)
            right = jnp.concatenate([theirs[t], theirs[t + 1]], axis=1)
            rest = jnp.dot(left[rows, depth:], right, preferred_element_type=F32)
            average = (part[rows, at] + rest) * (1.0 / ISLANDS)
            new = 0.9 * momentum[rows, at] + average
            sums[1, rows, at] = new
            sums[0, rows, at] = params[rows, at] - 0.7 * (average + 0.9 * new)
        for m, out in enumerate((new_params, new_momentum)):
            outs.append(pltpu.make_async_copy(sums.at[m, rows], out.at[rows], sems.at[m, n]))
            outs[-1].start()
    for out in outs:
        out.wait()


def update_call(params, momentum, part, left, theirs):
    shape = params.shape
    return pl.pallas_call(
        update_kernel,
        in_specs=[VMEM] * 5,
        out_specs=[FAR, FAR],
        out_shape=[jax.ShapeDtypeStruct(shape, F32)] * 2,
        scratch_shapes=[pltpu.VMEM((2,) + shape, F32), pltpu.SemaphoreType.DMA((2, 4))],
        compiler_params=pltpu.CompilerParams(vmem_limit_bytes=16 * 1024 * 1024),
        cost_estimate=pl.CostEstimate(flops=1100000000, bytes_accessed=14000000, transcendentals=0),
        name="update",
    )(left, theirs, part, params, momentum)


def body(delta, sketch, params, momentum):
    local = delta[0]
    rows, rank = local.shape[0], sketch.shape[1]
    depth = sketch.shape[0]
    x, yh, z, yl, core = (lax.axis_index(a) for a in AXES)
    fence = lax.optimization_barrier

    up = lambda v: move(v, lambda x, h, z, l, c: (x, h + l, z, l + 1, c))
    down = lambda v: move(v, lambda x, h, z, l, c: (x, h + l - 1, z, l - 1, c))
    swap = lambda vs: [shift(v, dc=1) for v in vs]
    near = [z, z - 1, z + 1, z - 2]
    starts = [
        (2 * (2 * (n % 4) + l) + c) * depth
        for c in (core, 1 - core)
        for n, l in ((z, yl), (z - 1, yl), (z + 1, yl), (z, 1 - yl), (z - 2, yl), (z - 2, 1 - yl))
    ]
    starts += [
        (2 * (2 * (n % 4) + 1 - yl) + c) * depth for c in (core, 1 - core) for n in (z - 1, z + 1)
    ]
    place = jnp.stack([core, 0, x, (core + yh) % 2] + starts).astype(jnp.int32)
    mid = depth // 2
    with jax.named_scope("gather_sketch"):
        z2 = shift(sketch, dz=2)
        z1, z3 = shift(sketch, dz=1), shift(sketch, dz=-1)
        pieces = [sketch, z1, z3, up(sketch), z2]
        y2 = [up(z2[:mid]), down(z2[mid:])]
        z1, z3, *y2 = fence((z1, z3, *y2))
        y1, y3 = up(z1), down(z3)
        pieces.append(jnp.concatenate(y2, 0))
        pieces += swap(pieces)
    part = call(
        functools.partial(early_kernel, range(4, 16)),
        [((rows, rank), F32)],
        1.6e9,
        "sketched_early",
    )(place, local, *pieces)[0]
    y1, y3, part = fence((y1, y3, part))
    with jax.named_scope("gather_sketch"):
        pieces = [y1, y3]
        pieces += swap(pieces)
    gram_part = ((BLK + BLK // 2, BLK), F32)
    mine, theirs, sketched, turned = call(
        functools.partial(late_kernel, range(16, 20)),
        [gram_part, gram_part, ((rows, rank), F32), ((rank, rows), BF16)],
        8e8,
        "sketched_late",
        scratch=[pltpu.VMEM((rows, rank), F32)],
    )(place, local, *pieces, part)

    with jax.named_scope("sum_gram"):
        mine = mine + shift(theirs, dc=1)
        mine, turned = fence((mine, turned))
        got = shift(mine, dl=1)
    shares = ((8, rank, 4 * BLK), BF16)
    sent, kept = call(
        product_kernel,
        [shares] * 2,
        2.2e9,
        "product",
        vmem=20,
    )(place, local, turned)
    got, sent, kept = fence((got, sent, kept))
    with jax.named_scope("sum_gram"):
        mine = mine + got
        got = [shift(mine, dz=d) for d in (2, 1, 3)]
    with jax.named_scope("sum_cores"):
        kept = (kept.astype(F32) + shift(sent, dc=1).astype(F32)).astype(BF16)
    *got, kept = fence((*got, kept))
    mine = (mine + got[0]) + (got[1] + got[2])
    mine, kept = fence((mine, kept))
    with jax.named_scope("sum_fsdp"):
        parts = lax.all_to_all(kept, ("z", "yl"), 0, 0, tiled=True)

    with jax.named_scope("sum_gram"):
        theirs = shift(mine, dc=1)
    inverse = call(
        inverse_kernel,
        [((rank, rank), F32)],
        3e9,
        "inverse",
        scratch=[pltpu.VMEM((rank, rank), F32)],
    )(place, mine, theirs)[0]
    basis = call(basis_kernel, [((rows, rank), BF16)], 4e8, "basis", False)(sketched, inverse)[0]
    with jax.named_scope("gather_basis"):
        across = shift(basis, dh=1)
    tiles = call(
        coef_kernel,
        [((rank, BLK), BF16)] * 4,
        4e8,
        "coef",
        scratch=[pltpu.VMEM((rank, 4 * BLK), BF16)],
    )(place, inverse, parts)
    *tiles, across = fence((*tiles, across))
    both = jnp.stack([basis, across])
    with jax.named_scope("gather_basis"):
        right, left = shift(both, dx=1), shift(both, dx=-1)
        far = jnp.stack([shift(right[0], dx=1), shift(left[1], dx=-1)])
    operand = call(lay_kernel, [((rows, 8 * rank), BF16)], 1e8, "lay")(
        place, both, right, far, left
    )[0]
    with jax.named_scope("exchange_coef"):
        tiles = [
            move(v, lambda x, h, z, l, c, d=d: (x + d, c, z, l, h)) for d, v in enumerate(tiles)
        ]
    tiles = call(spread_kernel, [pltpu.VMEM((8, 4 * rank, BLK), BF16)], 0, "spread", False)(*tiles)[0]
    with jax.named_scope("gather_coef"):
        mine, operand = fence((lax.all_to_all(tiles, ("z", "yl"), 0, 0, tiled=True), operand))
        theirs = shift(mine, dc=1)
    part = call(partial_kernel, [pltpu.VMEM((rows, 8 * BLK), F32)], 1.1e9, "partial", False)(operand, mine)[0]
    return tuple(update_call(params, momentum, part, operand, theirs))


def solution(mesh):
    mesh = Mesh(mesh.devices.reshape(SIZES), AXES)
    island, fsdp = AXES[:2], AXES[2:]
    placed = (P(island, fsdp, None), P(fsdp, None), P(fsdp, island), P(fsdp, island))
    return jax.shard_map(
        body,
        mesh=mesh,
        in_specs=placed,
        out_specs=(P(fsdp, island), P(fsdp, island)),
        check_vma=False,
    )
```

```python
import functools

import jax
import jax.numpy as jnp
import numpy as np
from jax import lax
from jax.experimental import pallas as pl
from jax.experimental.pallas import tpu as pltpu
from jax.sharding import Mesh, PartitionSpec as P

BLK = 128
AXES = ("x", "yh", "z", "yl", "core")
SIZES = (4, 2, 4, 2, 2)
ISLANDS = 8
HIGH = lax.Precision.HIGHEST
F32 = jnp.float32
BF16 = jnp.bfloat16


def move(value, where):
    pairs = []
    for c in np.ndindex(*SIZES):
        d = tuple(a % b for a, b in zip(where(*c), SIZES))
        pairs.append((int(np.ravel_multi_index(c, SIZES)), int(np.ravel_multi_index(d, SIZES))))
    return lax.ppermute(value, AXES, pairs)


def shift(value, dx=0, dh=0, dz=0, dl=0, dc=0):
    return move(value, lambda x, h, z, l, c: (x + dx, h + dh, z + dz, l + dl, c + dc))


def recode(values, axis):
    scale = (jnp.max(jnp.abs(values), axis=axis, keepdims=True) + 1e-06).astype(BF16).astype(F32)
    code = (values / scale).astype(BF16)
    return (code.astype(F32) * scale).astype(BF16)


VMEM = pl.BlockSpec(memory_space=pltpu.VMEM)
FAR = pl.BlockSpec(memory_space=pltpu.HBM)
SMEM = pl.BlockSpec(memory_space=pltpu.SMEM)


def call(kernel, outs, flops, name, smem=True, scratch=(), vmem=16):
    def run(*args):
        return pl.pallas_call(
            kernel,
            in_specs=[SMEM] * smem + [VMEM] * (len(args) - smem),
            out_specs=[VMEM] * len(outs),
            out_shape=[jax.ShapeDtypeStruct(*o) if isinstance(o, tuple) else o for o in outs],
            scratch_shapes=list(scratch),
            compiler_params=pltpu.CompilerParams(vmem_limit_bytes=vmem * 1024 * 1024),
            cost_estimate=pl.CostEstimate(
                flops=int(flops), bytes_accessed=4 * 1024 * 1024, transcendentals=0
            ),
            name=name,
        )(*args)

    return run


def columns(ref, start, count):
    return ref.at[:, pl.ds(pl.multiple_of(start, count), count)]


def add_products(layout, place, delta, pieces, out):
    for n, (piece, at) in enumerate(zip(pieces, layout)):
        value = jnp.dot(
            columns(delta, place[at], piece.shape[0])[...], piece[...], preferred_element_type=F32
        )
        if n == 0:
            out[...] = value
        else:
            out[...] += value


def early_kernel(layout, place, delta, *refs):
    add_products(layout, place, delta, refs[: len(layout)], refs[-1])


def late_kernel(layout, place, delta, *refs):
    pieces, part = refs[: len(layout)], refs[len(layout)]
    mine, theirs, rounded, turned, out = refs[len(layout) + 1 :]
    add_products(layout, place, delta, pieces, out)
    total = out[...] + part[...]
    flipped = total.T
    gram = jnp.dot(flipped, total, precision=HIGH, preferred_element_type=F32)
    rounded[...] = total.astype(BF16)
    turned[...] = flipped.astype(BF16)
    for core, to in ((0, (mine, theirs)), (1, (theirs, mine))):

        @pl.when(place[0] == core)
        def _(to=to):
            for n in range(2):
                at = n * BLK
                to[n][:BLK] = gram[at : at + BLK, at : at + BLK]
                to[n][BLK:] = gram[BLK + at // 2 : BLK + at // 2 + BLK // 2, :BLK]


def product_kernel(place, delta, turned, sent, kept):
    for out, parity in ((sent, 1 - place[0]), (kept, place[0])):
        for g in range(4):
            for q in range(2):
                tile = jnp.dot(
                    turned[...],
                    columns(delta, (2 * g + parity) * 1024 + q * 512, 512)[...],
                    preferred_element_type=F32,
                ).astype(BF16)
                for u in range(4):
                    out[4 * q + u, :, g * BLK : (g + 1) * BLK] = tile[:, u * BLK : (u + 1) * BLK]


def spread_kernel(first, *refs):
    tiles, (out, sems) = refs[:2], refs[-2:]
    rank = tiles[0].shape[0]
    copies = [
        pltpu.make_async_copy(
            tile, out.at[n, (first + d) * rank : (first + d + 1) * rank], sems.at[d, n]
        )
        for n in range(out.shape[0])
        for d, tile in enumerate(tiles)
    ]
    for copy in copies:
        copy.start()
    for copy in copies:
        copy.wait()


def spread_call(first, tiles, before=()):
    rank = tiles[0].shape[0]
    return pl.pallas_call(
        functools.partial(spread_kernel, first),
        in_specs=[VMEM, VMEM] + [FAR] * len(before),
        out_specs=FAR,
        out_shape=jax.ShapeDtypeStruct((8, 4 * rank, BLK), BF16),
        scratch_shapes=[pltpu.SemaphoreType.DMA((2, 8))],
        input_output_aliases={2: 0} if before else {},
        compiler_params=pltpu.CompilerParams(vmem_limit_bytes=4 * 1024 * 1024),
        cost_estimate=pl.CostEstimate(flops=0, bytes_accessed=1000000, transcendentals=0),
        name="spread",
    )(*tiles, *before)


def inverse_kernel(place, mine, theirs, out, left):
    size, wide = out.shape[0], 16
    half = BLK // 2
    for core, parts in ((0, (mine, theirs)), (1, (theirs, mine))):

        @pl.when(place[0] == core)
        def _(parts=parts):
            for n in range(2):
                at = n * BLK
                left[at : at + BLK, at : at + BLK] = parts[n][:BLK]
                left[BLK + n * half : BLK + (n + 1) * half, :BLK] = parts[n][BLK:]

    left[:BLK, BLK:] = left[BLK:, :BLK].T
    rows = lax.broadcasted_iota(jnp.int32, (size, size), 0)
    cols = lax.broadcasted_iota(jnp.int32, (size, size), 1)
    out[...] = (rows == cols).astype(F32)
    row = lax.broadcasted_iota(jnp.int32, (wide, BLK), 0)
    for k in range(0, size, wide):
        lo = k // BLK * BLK
        hi = lo + BLK
        over = lambda v, width: jnp.concatenate([v] * (width // BLK), 1)
        a, b = left[k : k + wide, lo:size], out[k : k + wide, :hi]
        col = [
            jnp.broadcast_to(left[k : k + wide, k + j : k + j + 1], (wide, BLK))
            for j in range(wide)
        ]
        done = []
        for i in range(wide):
            pivot = col[i][i : i + 1]
            root = lax.rsqrt(pivot)
            root = root * (1.5 - 0.5 * pivot * root * root)
            done.append(b[i : i + 1] * over(root, hi))
            inv = root * root
            factor = jnp.where(row == i, 1.0 - inv, col[i] * inv)
            for j in range(i + 1, wide):
                col[j] = col[j] - factor * col[j][i : i + 1]
            a = a - over(factor, size - lo) * a[i : i + 1]
            b = b - over(factor, hi) * b[i : i + 1]
        out[k : k + wide, :hi] = jnp.concatenate(done, 0)
        if k + wide < size:
            a_rest, b_rest = left[k + wide :, lo:size], out[k + wide :, :hi]
            for j in range(wide):
                c = left[k + wide :, k + j : k + j + 1]
                a_rest = a_rest - c * a[j : j + 1]
                b_rest = b_rest - c * b[j : j + 1]
            left[k + wide :, lo:size] = a_rest
            out[k + wide :, :hi] = b_rest


def coef_kernel(place, inverse, parts, *refs):
    outs, held = refs[:4], refs[4]
    total = parts[0].astype(F32)
    for t in range(1, 8):
        total += parts[t].astype(F32)
    coef = jnp.dot(inverse[...], total, precision=HIGH, preferred_element_type=F32)
    for b in range(2):
        held[b * BLK : (b + 1) * BLK] = recode(coef[b * BLK : (b + 1) * BLK], 0)
    for d in range(4):
        outs[d][...] = columns(held, (place[2] + d) % 4 * BLK, BLK)[...]


def basis_kernel(place, s0, s1, s2, s3, mine, theirs, left):
    for d, sketched in enumerate((s0, s1, s2, s3)):
        for n, yh in enumerate((place[3], 1 - place[3])):
            for core, inverse in ((place[0], mine), (1 - place[0], theirs)):
                basis = lax.dot_general(
                    sketched[yh],
                    inverse[d, yh],
                    (((1,), (1,)), ((), ())),
                    preferred_element_type=F32,
                )
                start = pl.multiple_of((2 * (4 * n + d) + core) * BLK, BLK)
                left[:, pl.ds(start, BLK)] = recode(basis, 1)


def partial_kernel(left, mine, out):
    depth = mine.shape[1]
    for t in range(0, 8, 2):
        right = jnp.concatenate([mine[t], mine[t + 1]], axis=1)
        out[:, t * BLK : (t + 2) * BLK] = jnp.dot(
            left[:, :depth], right, preferred_element_type=F32
        )


def update_kernel(left, theirs, part, params, momentum, new_params, new_momentum, sums, sems):
    depth = theirs.shape[1]
    steps = sems.shape[1]
    count = left.shape[0] // steps
    outs = []
    for n in range(steps):
        rows = slice(n * count, (n + 1) * count)
        for t in range(0, 8, 2):
            at = slice(t * BLK, (t + 2) * BLK)
            right = jnp.concatenate([theirs[t], theirs[t + 1]], axis=1)
            rest = jnp.dot(left[rows, depth:], right, preferred_element_type=F32)
            average = (part[rows, at] + rest) * (1.0 / ISLANDS)
            new = 0.9 * momentum[rows, at] + average
            sums[1, rows, at] = new
            sums[0, rows, at] = params[rows, at] - 0.7 * (average + 0.9 * new)
        for m, out in enumerate((new_params, new_momentum)):
            outs.append(pltpu.make_async_copy(sums.at[m, rows], out.at[rows], sems.at[m, n]))
            outs[-1].start()
    for out in outs:
        out.wait()


def update_call(params, momentum, part, left, theirs):
    shape = params.shape
    return pl.pallas_call(
        update_kernel,
        in_specs=[VMEM] * 5,
        out_specs=[FAR, FAR],
        out_shape=[jax.ShapeDtypeStruct(shape, F32)] * 2,
        scratch_shapes=[pltpu.VMEM((2,) + shape, F32), pltpu.SemaphoreType.DMA((2, 4))],
        compiler_params=pltpu.CompilerParams(vmem_limit_bytes=16 * 1024 * 1024),
        cost_estimate=pl.CostEstimate(flops=1100000000, bytes_accessed=14000000, transcendentals=0),
        name="update",
    )(left, theirs, part, params, momentum)


def body(delta, sketch, params, momentum):
    local = delta[0]
    rows, rank = local.shape[0], sketch.shape[1]
    depth = sketch.shape[0]
    x, yh, z, yl, core = (lax.axis_index(a) for a in AXES)
    fence = lax.optimization_barrier

    up = lambda v: move(v, lambda x, h, z, l, c: (x, h + l, z, l + 1, c))
    down = lambda v: move(v, lambda x, h, z, l, c: (x, h + l - 1, z, l - 1, c))
    swap = lambda vs: [shift(v, dc=1) for v in vs]
    near = [z, z - 1, z + 1, z - 2]
    starts = [
        (2 * (2 * (n % 4) + l) + c) * depth
        for c in (core, 1 - core)
        for n, l in ((z, yl), (z - 1, yl), (z + 1, yl), (z, 1 - yl), (z - 2, yl), (z - 2, 1 - yl))
    ]
    starts += [
        (2 * (2 * (n % 4) + 1 - yl) + c) * depth for c in (core, 1 - core) for n in (z - 1, z + 1)
    ]
    place = jnp.stack([core, 0, x, (core + yh) % 2] + starts).astype(jnp.int32)
    mid = depth // 2
    with jax.named_scope("gather_sketch"):
        z2 = shift(sketch, dz=2)
        z1, z3 = shift(sketch, dz=1), shift(sketch, dz=-1)
        pieces = [sketch, z1, z3, up(sketch), z2]
        y2 = [up(z2[:mid]), down(z2[mid:])]
        z1, z3, *y2 = fence((z1, z3, *y2))
        y1, y3 = up(z1), down(z3)
        pieces.append(jnp.concatenate(y2, 0))
        pieces += swap(pieces)
    part = call(
        functools.partial(early_kernel, range(4, 16)),
        [((rows, rank), F32)],
        1.6e9,
        "sketched_early",
    )(place, local, *pieces)[0]
    y1, y3, part = fence((y1, y3, part))
    with jax.named_scope("gather_sketch"):
        pieces = [y1, y3]
        pieces += swap(pieces)
    gram_part = ((BLK + BLK // 2, BLK), F32)
    mine, theirs, rounded, turned = call(
        functools.partial(late_kernel, range(16, 20)),
        [gram_part, gram_part, ((rows, rank), BF16), ((rank, rows), BF16)],
        8e8,
        "sketched_late",
        scratch=[pltpu.VMEM((rows, rank), F32)],
    )(place, local, *pieces, part)

    with jax.named_scope("sum_gram"):
        mine = mine + shift(theirs, dc=1)
        mine, turned = fence((mine, turned))
        got = shift(mine, dl=1)
    shares = ((8, rank, 4 * BLK), BF16)
    sent, kept = call(
        product_kernel,
        [shares] * 2,
        2.2e9,
        "product",
        vmem=20,
    )(place, local, turned)
    got, sent, kept = fence((got, sent, kept))
    with jax.named_scope("sum_gram"):
        mine = mine + got
        got = [shift(mine, dz=d) for d in (2, 1, 3)]
    with jax.named_scope("sum_cores"):
        kept = (kept.astype(F32) + shift(sent, dc=1).astype(F32)).astype(BF16)
    with jax.named_scope("gather_sketched"):
        across = shift(rounded, dh=1)
    *got, kept, across = fence((*got, kept, across))
    mine = (mine + got[0]) + (got[1] + got[2])
    mine, kept = fence((mine, kept))
    with jax.named_scope("gather_sketched"):
        both = jnp.stack([rounded, across])
        right, left = shift(both, dx=1), shift(both, dx=-1)
    with jax.named_scope("sum_fsdp"):
        parts = lax.all_to_all(kept, ("z", "yl"), 0, 0, tiled=True)

    with jax.named_scope("sum_gram"):
        theirs = shift(mine, dc=1)
    inverse = call(
        inverse_kernel,
        [((rank, rank), F32)],
        3e9,
        "inverse",
        scratch=[pltpu.VMEM((rank, rank), F32)],
    )(place, mine, theirs)[0]
    inverse, right, left = fence((inverse, right, left))
    with jax.named_scope("gather_sketched"):
        far = [shift(right[0], dx=1), shift(left[1], dx=-1)]
    with jax.named_scope("gather_inverse"):
        half_inverse = lax.dynamic_slice_in_dim(inverse, core * BLK, BLK, 0).astype(BF16)
        across = shift(half_inverse, dh=1)
    tiles = call(
        coef_kernel,
        [((rank, BLK), BF16)] * 4,
        4e8,
        "coef",
        scratch=[pltpu.VMEM((rank, 4 * BLK), BF16)],
    )(place, inverse, parts)
    *tiles, across, far[0], far[1] = fence((*tiles, across, *far))
    with jax.named_scope("gather_inverse"):
        pair = jnp.stack([half_inverse, across])
        inverses = jnp.stack([pair] + [shift(pair, dx=d) for d in range(1, 4)])
        other = shift(inverses, dc=1)
    operand = call(basis_kernel, [((rows, 8 * rank), BF16)], 5.4e8, "basis")(
        place, both, right, jnp.stack(far), left, inverses, other
    )[0]
    with jax.named_scope("exchange_coef"):
        tiles = [
            move(v, lambda x, h, z, l, c, d=d: (x + d, c, z, l, h)) for d, v in enumerate(tiles)
        ]
    half = spread_call(0, tiles[:2])
    *rest, half = fence((*tiles[2:], half))
    tiles = spread_call(2, rest, (half,))
    with jax.named_scope("gather_coef"):
        mine, operand = fence((lax.all_to_all(tiles, ("z", "yl"), 0, 0, tiled=True), operand))
        theirs = shift(mine, dc=1)
    part = call(partial_kernel, [pltpu.VMEM((rows, 8 * BLK), F32)], 1.1e9, "partial", False)(operand, mine)[0]
    return tuple(update_call(params, momentum, part, operand, theirs))


def solution(mesh):
    mesh = Mesh(mesh.devices.reshape(SIZES), AXES)
    island, fsdp = AXES[:2], AXES[2:]
    placed = (P(island, fsdp, None), P(fsdp, None), P(fsdp, island), P(fsdp, island))
    return jax.shard_map(
        body,
        mesh=mesh,
        in_specs=placed,
        out_specs=(P(fsdp, island), P(fsdp, island)),
        check_vma=False,
    )
```

```python
import functools

import jax
import jax.numpy as jnp
import numpy as np
from jax import lax
from jax.experimental import pallas as pl
from jax.experimental.pallas import tpu as pltpu
from jax.sharding import Mesh, PartitionSpec as P

BLK = 128
AXES = ("x", "yh", "z", "yl", "core")
SIZES = (4, 2, 4, 2, 2)
ISLANDS = 8
HIGH = lax.Precision.HIGHEST
F32 = jnp.float32
BF16 = jnp.bfloat16


def move(value, where):
    pairs = []
    for c in np.ndindex(*SIZES):
        d = tuple(a % b for a, b in zip(where(*c), SIZES))
        pairs.append((int(np.ravel_multi_index(c, SIZES)), int(np.ravel_multi_index(d, SIZES))))
    return lax.ppermute(value, AXES, pairs)


def shift(value, dx=0, dh=0, dz=0, dl=0, dc=0):
    return move(value, lambda x, h, z, l, c: (x + dx, h + dh, z + dz, l + dl, c + dc))


def recode(values, axis):
    scale = (jnp.max(jnp.abs(values), axis=axis, keepdims=True) + 1e-06).astype(BF16).astype(F32)
    code = (values / scale).astype(BF16)
    return (code.astype(F32) * scale).astype(BF16)


VMEM = pl.BlockSpec(memory_space=pltpu.VMEM)
FAR = pl.BlockSpec(memory_space=pltpu.HBM)
SMEM = pl.BlockSpec(memory_space=pltpu.SMEM)


def call(kernel, outs, flops, name, smem=True, scratch=(), vmem=16):
    def run(*args):
        return pl.pallas_call(
            kernel,
            in_specs=[SMEM] * smem + [VMEM] * (len(args) - smem),
            out_specs=[VMEM] * len(outs),
            out_shape=[jax.ShapeDtypeStruct(*o) if isinstance(o, tuple) else o for o in outs],
            scratch_shapes=list(scratch),
            compiler_params=pltpu.CompilerParams(vmem_limit_bytes=vmem * 1024 * 1024),
            cost_estimate=pl.CostEstimate(
                flops=int(flops), bytes_accessed=4 * 1024 * 1024, transcendentals=0
            ),
            name=name,
        )(*args)

    return run


def columns(ref, start, count):
    return ref.at[:, pl.ds(pl.multiple_of(start, count), count)]


def add_products(layout, place, delta, pieces, out):
    for n, (piece, at) in enumerate(zip(pieces, layout)):
        value = jnp.dot(
            columns(delta, place[at], piece.shape[0])[...], piece[...], preferred_element_type=F32
        )
        if n == 0:
            out[...] = value
        else:
            out[...] += value


def early_kernel(layout, place, delta, *refs):
    add_products(layout, place, delta, refs[: len(layout)], refs[-1])


def late_kernel(layout, place, delta, *refs):
    pieces, part = refs[: len(layout)], refs[len(layout)]
    mine, theirs, sketched, turned, out = refs[len(layout) + 1 :]
    add_products(layout, place, delta, pieces, out)
    total = out[...] + part[...]
    flipped = total.T
    gram = jnp.dot(flipped, total, precision=HIGH, preferred_element_type=F32)
    sketched[...] = total
    turned[...] = flipped.astype(BF16)
    for core, to in ((0, (mine, theirs)), (1, (theirs, mine))):

        @pl.when(place[0] == core)
        def _(to=to):
            for n in range(2):
                at = n * BLK
                to[n][:BLK] = gram[at : at + BLK, at : at + BLK]
                to[n][BLK:] = gram[BLK + at // 2 : BLK + at // 2 + BLK // 2, :BLK]


def product_kernel(place, delta, turned, sent, kept):
    for out, parity in ((sent, 1 - place[0]), (kept, place[0])):
        for g in range(4):
            for q in range(2):
                tile = jnp.dot(
                    turned[...],
                    columns(delta, (2 * g + parity) * 1024 + q * 512, 512)[...],
                    preferred_element_type=F32,
                ).astype(BF16)
                for u in range(4):
                    out[4 * q + u, :, g * BLK : (g + 1) * BLK] = tile[:, u * BLK : (u + 1) * BLK]


def spread_kernel(first, *refs):
    tiles, (out, sems) = refs[:2], refs[-2:]
    rank = tiles[0].shape[0]
    copies = [
        pltpu.make_async_copy(
            tile, out.at[n, (first + d) * rank : (first + d + 1) * rank], sems.at[d, n]
        )
        for n in range(out.shape[0])
        for d, tile in enumerate(tiles)
    ]
    for copy in copies:
        copy.start()
    for copy in copies:
        copy.wait()


def spread_call(first, tiles, before=()):
    rank = tiles[0].shape[0]
    return pl.pallas_call(
        functools.partial(spread_kernel, first),
        in_specs=[VMEM, VMEM] + [FAR] * len(before),
        out_specs=FAR,
        out_shape=jax.ShapeDtypeStruct((8, 4 * rank, BLK), BF16),
        scratch_shapes=[pltpu.SemaphoreType.DMA((2, 8))],
        input_output_aliases={2: 0} if before else {},
        compiler_params=pltpu.CompilerParams(vmem_limit_bytes=4 * 1024 * 1024),
        cost_estimate=pl.CostEstimate(flops=0, bytes_accessed=1000000, transcendentals=0),
        name="spread",
    )(*tiles, *before)


def inverse_kernel(place, mine, theirs, out, left):
    size, wide = out.shape[0], 16
    half = BLK // 2
    for core, parts in ((0, (mine, theirs)), (1, (theirs, mine))):

        @pl.when(place[0] == core)
        def _(parts=parts):
            for n in range(2):
                at = n * BLK
                left[at : at + BLK, at : at + BLK] = parts[n][:BLK]
                left[BLK + n * half : BLK + (n + 1) * half, :BLK] = parts[n][BLK:]

    left[:BLK, BLK:] = left[BLK:, :BLK].T
    rows = lax.broadcasted_iota(jnp.int32, (size, size), 0)
    cols = lax.broadcasted_iota(jnp.int32, (size, size), 1)
    out[...] = (rows == cols).astype(F32)
    row = lax.broadcasted_iota(jnp.int32, (wide, BLK), 0)
    for k in range(0, size, wide):
        lo = k // BLK * BLK
        hi = lo + BLK
        over = lambda v, width: jnp.concatenate([v] * (width // BLK), 1)
        a, b = left[k : k + wide, lo:size], out[k : k + wide, :hi]
        col = [
            jnp.broadcast_to(left[k : k + wide, k + j : k + j + 1], (wide, BLK))
            for j in range(wide)
        ]
        done = []
        for i in range(wide):
            pivot = col[i][i : i + 1]
            root = lax.rsqrt(pivot)
            root = root * (1.5 - 0.5 * pivot * root * root)
            done.append(b[i : i + 1] * over(root, hi))
            inv = root * root
            factor = jnp.where(row == i, 1.0 - inv, col[i] * inv)
            for j in range(i + 1, wide):
                col[j] = col[j] - factor * col[j][i : i + 1]
            a = a - over(factor, size - lo) * a[i : i + 1]
            b = b - over(factor, hi) * b[i : i + 1]
        out[k : k + wide, :hi] = jnp.concatenate(done, 0)
        if k + wide < size:
            a_rest, b_rest = left[k + wide :, lo:size], out[k + wide :, :hi]
            for j in range(wide):
                c = left[k + wide :, k + j : k + j + 1]
                a_rest = a_rest - c * a[j : j + 1]
                b_rest = b_rest - c * b[j : j + 1]
            left[k + wide :, lo:size] = a_rest
            out[k + wide :, :hi] = b_rest


def coef_kernel(place, inverse, parts, *refs):
    outs, held = refs[:4], refs[4]
    total = parts[0].astype(F32)
    for t in range(1, 8):
        total += parts[t].astype(F32)
    coef = jnp.dot(inverse[...], total, precision=HIGH, preferred_element_type=F32)
    for b in range(2):
        held[b * BLK : (b + 1) * BLK] = recode(coef[b * BLK : (b + 1) * BLK], 0)
    for d in range(4):
        outs[d][...] = columns(held, (place[2] + d) % 4 * BLK, BLK)[...]


def basis_kernel(sketched, inverse, out):
    basis = lax.dot_general(
        sketched[...],
        inverse[...],
        (((1,), (1,)), ((), ())),
        precision=HIGH,
        preferred_element_type=F32,
    )
    for b in range(2):
        out[:, b * BLK : (b + 1) * BLK] = recode(basis[:, b * BLK : (b + 1) * BLK], 1)


def lay_kernel(place, q0, q1, q2, q3, left):
    rank = q0.shape[2]
    for d, q in enumerate((q0, q1, q2, q3)):
        left[:, d * rank : (d + 1) * rank] = q[place[3]]
        left[:, (4 + d) * rank : (5 + d) * rank] = q[1 - place[3]]


def partial_kernel(left, mine, out):
    depth = mine.shape[1]
    for t in range(0, 8, 2):
        right = jnp.concatenate([mine[t], mine[t + 1]], axis=1)
        out[:, t * BLK : (t + 2) * BLK] = jnp.dot(
            left[:, :depth], right, preferred_element_type=F32
        )


def update_kernel(left, theirs, part, params, momentum, new_params, new_momentum, sums, sems):
    depth = theirs.shape[1]
    steps = sems.shape[1]
    count = left.shape[0] // steps
    outs = []
    for n in range(steps):
        rows = slice(n * count, (n + 1) * count)
        for t in range(0, 8, 2):
            at = slice(t * BLK, (t + 2) * BLK)
            right = jnp.concatenate([theirs[t], theirs[t + 1]], axis=1)
            rest = jnp.dot(left[rows, depth:], right, preferred_element_type=F32)
            average = (part[rows, at] + rest) * (1.0 / ISLANDS)
            new = 0.9 * momentum[rows, at] + average
            sums[1, rows, at] = new
            sums[0, rows, at] = params[rows, at] - 0.7 * (average + 0.9 * new)
        for m, out in enumerate((new_params, new_momentum)):
            outs.append(pltpu.make_async_copy(sums.at[m, rows], out.at[rows], sems.at[m, n]))
            outs[-1].start()
    for out in outs:
        out.wait()


def update_call(params, momentum, part, left, theirs):
    shape = params.shape
    return pl.pallas_call(
        update_kernel,
        in_specs=[VMEM] * 5,
        out_specs=[FAR, FAR],
        out_shape=[jax.ShapeDtypeStruct(shape, F32)] * 2,
        scratch_shapes=[pltpu.VMEM((2,) + shape, F32), pltpu.SemaphoreType.DMA((2, 4))],
        compiler_params=pltpu.CompilerParams(vmem_limit_bytes=16 * 1024 * 1024),
        cost_estimate=pl.CostEstimate(flops=1100000000, bytes_accessed=14000000, transcendentals=0),
        name="update",
    )(left, theirs, part, params, momentum)


def body(delta, sketch, params, momentum):
    local = delta[0]
    rows, rank = local.shape[0], sketch.shape[1]
    depth = sketch.shape[0]
    x, yh, z, yl, core = (lax.axis_index(a) for a in AXES)
    fence = lax.optimization_barrier

    up = lambda v: move(v, lambda x, h, z, l, c: (x, h + l, z, l + 1, c))
    down = lambda v: move(v, lambda x, h, z, l, c: (x, h + l - 1, z, l - 1, c))
    swap = lambda vs: [shift(v, dc=1) for v in vs]
    near = [z, z - 1, z + 1, z - 2]
    starts = [
        (2 * (2 * (n % 4) + l) + c) * depth
        for c in (core, 1 - core)
        for n, l in ((z, yl), (z - 1, yl), (z + 1, yl), (z, 1 - yl), (z - 2, yl), (z - 2, 1 - yl))
    ]
    starts += [
        (2 * (2 * (n % 4) + 1 - yl) + c) * depth for c in (core, 1 - core) for n in (z - 1, z + 1)
    ]
    place = jnp.stack([core, 0, x, (core + yh) % 2] + starts).astype(jnp.int32)
    mid = depth // 2
    with jax.named_scope("gather_sketch"):
        z2 = shift(sketch, dz=2)
        z1, z3 = shift(sketch, dz=1), shift(sketch, dz=-1)
        pieces = [sketch, z1, z3, up(sketch), z2]
        y2 = [up(z2[:mid]), down(z2[mid:])]
        z1, z3, *y2 = fence((z1, z3, *y2))
        y1, y3 = up(z1), down(z3)
        pieces.append(jnp.concatenate(y2, 0))
        pieces += swap(pieces)
    part = call(
        functools.partial(early_kernel, range(4, 16)),
        [((rows, rank), F32)],
        1.6e9,
        "sketched_early",
    )(place, local, *pieces)[0]
    y1, y3, part = fence((y1, y3, part))
    with jax.named_scope("gather_sketch"):
        pieces = [y1, y3]
        pieces += swap(pieces)
    gram_part = ((BLK + BLK // 2, BLK), F32)
    mine, theirs, sketched, turned = call(
        functools.partial(late_kernel, range(16, 20)),
        [gram_part, gram_part, ((rows, rank), F32), ((rank, rows), BF16)],
        8e8,
        "sketched_late",
        scratch=[pltpu.VMEM((rows, rank), F32)],
    )(place, local, *pieces, part)

    with jax.named_scope("sum_gram"):
        mine = mine + shift(theirs, dc=1)
        mine, turned = fence((mine, turned))
        got = shift(mine, dl=1)
    shares = ((8, rank, 4 * BLK), BF16)
    sent, kept = call(
        product_kernel,
        [shares] * 2,
        2.2e9,
        "product",
        vmem=20,
    )(place, local, turned)
    got, sent, kept = fence((got, sent, kept))
    with jax.named_scope("sum_gram"):
        mine = mine + got
        got = [shift(mine, dz=d) for d in (2, 1, 3)]
    with jax.named_scope("sum_cores"):
        kept = (kept.astype(F32) + shift(sent, dc=1).astype(F32)).astype(BF16)
    *got, kept = fence((*got, kept))
    mine = (mine + got[0]) + (got[1] + got[2])
    mine, kept = fence((mine, kept))
    with jax.named_scope("sum_fsdp"):
        parts = lax.all_to_all(kept, ("z", "yl"), 0, 0, tiled=True)

    with jax.named_scope("sum_gram"):
        theirs = shift(mine, dc=1)
    inverse = call(
        inverse_kernel,
        [((rank, rank), F32)],
        3e9,
        "inverse",
        scratch=[pltpu.VMEM((rank, rank), F32)],
    )(place, mine, theirs)[0]
    basis = call(basis_kernel, [((rows, rank), BF16)], 4e8, "basis", False)(sketched, inverse)[0]
    with jax.named_scope("gather_basis"):
        across = shift(basis, dh=1)
    tiles = call(
        coef_kernel,
        [((rank, BLK), BF16)] * 4,
        4e8,
        "coef",
        scratch=[pltpu.VMEM((rank, 4 * BLK), BF16)],
    )(place, inverse, parts)
    *tiles, across = fence((*tiles, across))
    both = jnp.stack([basis, across])
    with jax.named_scope("gather_basis"):
        right, left = shift(both, dx=1), shift(both, dx=-1)
        far = jnp.stack([shift(right[0], dx=1), shift(left[1], dx=-1)])
    operand = call(lay_kernel, [((rows, 8 * rank), BF16)], 1e8, "lay")(
        place, both, right, far, left
    )[0]
    with jax.named_scope("exchange_coef"):
        tiles = [
            move(v, lambda x, h, z, l, c, d=d: (x + d, c, z, l, h)) for d, v in enumerate(tiles)
        ]
    half = spread_call(0, tiles[:2])
    *rest, half = fence((*tiles[2:], half))
    tiles = spread_call(2, rest, (half,))
    with jax.named_scope("gather_coef"):
        mine, operand = fence((lax.all_to_all(tiles, ("z", "yl"), 0, 0, tiled=True), operand))
        theirs = shift(mine, dc=1)
    part = call(partial_kernel, [pltpu.VMEM((rows, 8 * BLK), F32)], 1.1e9, "partial", False)(operand, mine)[0]
    return tuple(update_call(params, momentum, part, operand, theirs))


def solution(mesh):
    mesh = Mesh(mesh.devices.reshape(SIZES), AXES)
    island, fsdp = AXES[:2], AXES[2:]
    placed = (P(island, fsdp, None), P(fsdp, None), P(fsdp, island), P(fsdp, island))
    return jax.shard_map(
        body,
        mesh=mesh,
        in_specs=placed,
        out_specs=(P(fsdp, island), P(fsdp, island)),
        check_vma=False,
    )
```
